32 devices in a mesh: obj: 2 (over x), dp: 4 (over y, core), tensor: 4 (over z).
Axes of the slice: x: 2, y: 2, z: 4, core: 2. Of those that a mesh axis runs over, the one named last changes fastest.
Arguments:
- tokens: bfloat16 [2, 8, 1024, 2048], P('obj', 'dp', 'tensor'), may hold values from -6 to 6
- cotangent: bfloat16 [2, 8, 1024, 2048], P('obj', 'dp', 'tensor'), may hold values from -6 to 6
- loss_mask: int32 [2, 8, 1024], P('obj', 'dp', 'tensor'), may hold values 0 or 1
- prefix: int32 [8], P('dp'), may hold values from 1 to 1023
- counts: int32 [2], replicated, may hold values from 256 to 8191
- w_qkv: bfloat16 [2048, 16, 384], P('dp', 'tensor'), may hold values from -0.125 to 0.125
- b_qkv: bfloat16 [16, 384], P('tensor'), may hold values from -1.75 to 1.75
- w_dense: bfloat16 [16, 128, 2048], P('tensor', None, 'dp'), may hold values from -2.5 to 2.5
- b_dense: bfloat16 [2048], replicated, may hold values from -3 to 3
- ln1_gain: bfloat16 [2048], replicated, may hold values from 0.099609375 to 1.8984375
- ln1_bias: bfloat16 [2048], replicated, may hold values from -3 to 3
- w_up: bfloat16 [2, 2048, 5632], P(None, 'dp', 'tensor'), may hold values from -0.125 to 0.125
- b_up: bfloat16 [2, 5632], P(None, 'tensor'), may hold values from -3 to 3
- w_down: bfloat16 [5632, 2048], P('tensor', 'dp'), may hold values from -0.625 to 0.625
- b_down: bfloat16 [2048], replicated, may hold values from -3 to 3
- ln2_gain: bfloat16 [2048], replicated, may hold values from 0.099609375 to 1.8984375
- ln2_bias: bfloat16 [2048], replicated, may hold values from -3 to 3
Outputs:
- layer_out: bfloat16 [2, 8, 1024, 2048], P('obj', 'dp', 'tensor')
- grad_tokens: float32 [2, 8, 1024, 2048], P('obj', 'dp', 'tensor')
- grad_w_qkv: float32 [2048, 16, 384], P('dp', 'tensor')
- grad_b_qkv: float32 [16, 384], P('tensor')
- grad_w_dense: float32 [16, 128, 2048], P('tensor', None, 'dp')
- grad_b_dense: float32 [2048], replicated
- grad_ln1_gain: float32 [2048], replicated
- grad_ln1_bias: float32 [2048], replicated
- grad_w_up: float32 [2, 2048, 5632], P(None, 'dp', 'tensor')
- grad_b_up: float32 [2, 5632], P(None, 'tensor')
- grad_w_down: float32 [5632, 2048], P('tensor', 'dp')
- grad_b_down: float32 [2048], replicated
- grad_ln2_gain: float32 [2048], replicated
- grad_ln2_bias: float32 [2048], replicated
The draws below stay inside these ranges and needn't reach their ends.
Inputs may be any that keep to these rules, and one draw needn't show every extreme that they name: prefix holds the prefix length of GLM item i: a query at position p of that item sees key q when q < prefix or q <= p; MLM items see every key. counts weigh the two groups in the loss.
All inputs are finite; a program needn't handle non-finite values. No bound on the sum of `loss_mask` on one device may be relied on, other than what follows from the above.
Results may differ from the reference program's by a relative error of at most 0.02.
Values may be sent and summed in bfloat16 or wider, within the bound.
No kernel may reach another device: no remote copies, remote signals or barrier semaphores. Data moves between devices by JAX's collectives and lax.ppermute only.
A program may use at most 320 MiB of HBM per device.

```python
import jax
import jax.numpy as jnp
from jax import lax

D = 2048
H = 16
HD = 128
FF = 5632
SEQ = 1024
NITEMS = 8
N_OBJ = 2


def touch_ends(result, key, smallest, top_value):
    dims = result.shape
    index_at = [jax.random.randint(jax.random.fold_in(key, axis), (), 0, dims[axis]) for axis in range(len(dims))]
    result = result.at[tuple(index_at)].set(smallest)
    longest = dims.index(max(dims))
    index_at[longest] = (index_at[longest] + 1) % dims[longest]
    return result.at[tuple(index_at)].set(top_value)


def levels(own_key, dims, cuts, smallest, top_value):
    def one(position, blocks):
        heights = jax.random.uniform(jax.random.fold_in(jax.random.fold_in(own_key, 6), position), (blocks,), jnp.float32, smallest / len(cuts), top_value / len(cuts))
        return jnp.repeat(jnp.exp(heights), dims[position] // blocks).reshape((-1,) + (1,) * (len(dims) - position - 1))

    gain = one(*cuts[0])
    for cut in cuts[1:]:
        gain = gain * one(*cut)
    return gain


def normal_values(own_key, shape, spread, reach, split=(), kind=jnp.bfloat16):
    level = levels(own_key, shape, split, -0.22, 0.18) if split else 1.0
    result = jax.random.normal(own_key, shape, jnp.float32) * spread * level
    return jnp.minimum(jnp.maximum(result, -reach), reach).astype(kind)


def setup_inputs(seed: int = 0) -> dict:
    key_list = jax.random.split(jax.random.key(seed), 18)
    tokens = normal_values(key_list[0], (N_OBJ, NITEMS, SEQ, D), 1.0, 6.0, ((0, 2), (1, 4), (2, 4)))
    cotangent = normal_values(key_list[1], (N_OBJ, NITEMS, SEQ, D), 1.0, 6.0, ((0, 2), (1, 4), (2, 4)))
    loss_mask = touch_ends((jax.random.randint(key_list[2], (N_OBJ, NITEMS, SEQ), 0, 4) < 3).astype(jnp.int32), jax.random.fold_in(key_list[2], 1), 0, 1)
    prefix = touch_ends(jax.random.randint(key_list[3], (NITEMS,), 1, SEQ), jax.random.fold_in(key_list[3], 1), 1, SEQ - 1).astype(jnp.int32)
    counts = jax.random.randint(key_list[4], (N_OBJ,), 256, 8192).astype(jnp.int32)
    w_qkv = normal_values(key_list[5], (D, H, 3 * HD), D ** -0.5, 0.125, ((0, 4), (1, 4)))
    b_qkv = normal_values(key_list[6], (H, 3 * HD), 0.3, 1.75, ((0, 4),))
    w_dense = normal_values(key_list[7], (H, HD, D), (20.0 / (H * HD) ** 0.5), 2.5, ((0, 4), (2, 4)))
    b_dense = normal_values(key_list[8], (D,), 0.5, 3.0)
    ln1_gain = jnp.clip(1.0 + 0.18 * jax.random.normal(key_list[9], (D,), jnp.float32), 0.099609375, 1.8984375).astype(jnp.bfloat16)
    ln1_bias = normal_values(key_list[10], (D,), 0.5, 3.0)
    w_up = normal_values(key_list[11], (2, D, FF), D ** -0.5, 0.125, ((1, 4), (2, 4)))
    b_up = normal_values(key_list[12], (2, FF), 0.5, 3.0, ((1, 4),))
    w_down = normal_values(key_list[13], (FF, D), (8.0 / FF ** 0.5), 0.625, ((0, 4), (1, 4)))
    b_down = normal_values(key_list[14], (D,), 0.5, 3.0)
    ln2_gain = jnp.clip(1.0 + 0.18 * jax.random.normal(key_list[15], (D,), jnp.float32), 0.099609375, 1.8984375).astype(jnp.bfloat16)
    ln2_bias = normal_values(key_list[16], (D,), 0.5, 3.0)
    return {"tokens": tokens, "cotangent": cotangent, "loss_mask": loss_mask, "prefix": prefix, "counts": counts, "w_qkv": w_qkv, "b_qkv": b_qkv, "w_dense": w_dense, "b_dense": b_dense, "ln1_gain": ln1_gain, "ln1_bias": ln1_bias, "w_up": w_up, "b_up": b_up, "w_down": w_down, "b_down": b_down, "ln2_gain": ln2_gain, "ln2_bias": ln2_bias}


ALPHA = 48.0 ** 0.5
epsilon = 1e-05
highest = lax.Precision.HIGHEST

@jax.custom_vjp
def low(v):
    return lax.optimization_barrier(v.astype(jnp.bfloat16)).astype(jnp.float32)

@jax.custom_vjp
def low_back(v):
    return v

def low_keep(v):
    return (low(v), None)

def low_pass(kept, grad):
    return (grad,)

def back_keep(v):
    return (v, None)

def back_low(kept, grad):
    return (low(grad),)
low.defvjp(low_keep, low_pass)
low_back.defvjp(back_keep, back_low)

def rotary(source):
    length = source.shape[0]
    half_dim = source.shape[-1] // 2
    frequency = 10000.0 ** (-2.0 * jnp.arange(half_dim, dtype=jnp.float32) / source.shape[-1])
    angles = jnp.arange(length, dtype=jnp.float32)[:, None] * frequency[None, :]
    cosine = jnp.cos(angles)[:, None, :]
    sine_table = jnp.sin(angles)[:, None, :]
    first_half = source[..., :half_dim]
    second = source[..., half_dim:]
    return jnp.concatenate([first_half * cosine - second * sine_table, second * cosine + first_half * sine_table], axis=-1)

def layer_norm(source, gain_vec, shift_vec):
    centred = source - lax.optimization_barrier(jnp.mean(source, axis=-1, keepdims=True))
    variance = lax.optimization_barrier(jnp.mean(centred * centred, axis=-1, keepdims=True))
    return centred * lax.rsqrt(variance + epsilon) * gain_vec + shift_vec

def attention(queries, keys_all, values_all, prefix_length):
    length = queries.shape[0]
    block_rows = min(512, length)
    block_count = length // block_rows
    score_scale = queries.shape[-1] ** (-0.5)

    def one_block(start):
        query_block = lax.dynamic_slice_in_dim(queries, start, block_rows, 0)
        scores = jnp.einsum('qhd,khd->hqk', query_block, keys_all, precision=highest) * score_scale
        scores = low_back(scores)
        query_pos = start + jnp.arange(block_rows, dtype=jnp.int32)
        key_pos = jnp.arange(length, dtype=jnp.int32)
        visible = (key_pos[None, :] < prefix_length) | (key_pos[None, :] <= query_pos[:, None])
        attn_weights = jax.nn.softmax(jnp.where(visible[None], scores, -1e+30), axis=-1)
        return jnp.einsum('hqk,khd->qhd', low(attn_weights), values_all, precision=highest)
    starts = jnp.arange(block_count, dtype=jnp.int32) * block_rows
    blocks = lax.map(jax.checkpoint(one_block), starts)
    return blocks.reshape(length, queries.shape[1], queries.shape[2])

def forward(source, params, prefix_length):
    w_qkv, b_qkv, w_dense, b_dense, ln1_gain, ln1_bias, w_up, b_up, w_down, b_down, ln2_gain, ln2_bias = params
    head_dim = w_qkv.shape[2] // 3
    projected = low_back(jnp.einsum('ld,dhe->lhe', low(source), w_qkv, precision=highest) + b_qkv)
    queries = low(rotary(projected[..., :head_dim]))
    keys_all = low(rotary(projected[..., head_dim:2 * head_dim]))
    values_all = low(projected[..., 2 * head_dim:])
    context = low(low_back(attention(queries, keys_all, values_all, prefix_length)))
    attn_out = low_back(jnp.einsum('lhd,hde->le', context, w_dense, precision=highest) + b_dense)
    first_norm = layer_norm(ALPHA * source + attn_out, ln1_gain, ln1_bias)
    gate_up = low_back(jnp.einsum('ld,kdf->klf', low(first_norm), w_up, precision=highest) + b_up[:, None, :])
    hidden = low(jax.nn.gelu(gate_up[0]) * gate_up[1])
    mlp_out = low_back(jnp.dot(hidden, w_down, precision=highest) + b_down)
    return layer_norm(ALPHA * first_norm + mlp_out, ln2_gain, ln2_bias)

def reference(tokens, cotangent, loss_mask, prefix, counts, w_qkv, b_qkv, w_dense, b_dense, ln1_gain, ln1_bias, w_up, b_up, w_down, b_down, ln2_gain, ln2_bias):
    params = tuple((parameter.astype(jnp.float32) for parameter in (w_qkv, b_qkv, w_dense, b_dense, ln1_gain, ln1_bias, w_up, b_up, w_down, b_down, ln2_gain, ln2_bias)))
    count_float = counts.astype(jnp.float32)
    shares = count_float / (count_float[0] + count_float[1])
    flat_tokens = tokens.reshape(N_OBJ * NITEMS, SEQ, D)
    flat_cotangent = cotangent.reshape(N_OBJ * NITEMS, SEQ, D)
    flat_mask = loss_mask.reshape(N_OBJ * NITEMS, SEQ)

    def one_item(totals, item_index):
        group_id = item_index // NITEMS
        item_slot = item_index % NITEMS
        prefix_length = jnp.where(group_id == 0, SEQ, prefix[item_slot]).astype(jnp.int32)
        source = flat_tokens[item_index].astype(jnp.float32)
        weight = flat_cotangent[item_index].astype(jnp.float32) * flat_mask[item_index].astype(jnp.float32)[:, None] * shares[group_id]
        output, pullback = jax.vjp(lambda source_in, weight_set: forward(source_in, weight_set, prefix_length), source, params)
        grad_source, grad_params = pullback(weight)
        totals = jax.tree.map(lambda running, fresh: running + fresh, totals, grad_params)
        return (totals, (output.astype(jnp.bfloat16), grad_source))
    zero_grads = jax.tree.map(jnp.zeros_like, params)
    totals, (outputs, grad_tokens) = lax.scan(one_item, zero_grads, jnp.arange(N_OBJ * NITEMS, dtype=jnp.int32))
    return (outputs.reshape(N_OBJ, NITEMS, SEQ, D), grad_tokens.reshape(N_OBJ, NITEMS, SEQ, D), totals[0], totals[1], totals[2], totals[3], totals[4], totals[5], totals[6], totals[7], totals[8], totals[9], totals[10], totals[11])
```

```python
import math

import jax
import jax.numpy as jnp
from jax import lax
from jax.experimental import pallas as pl
from jax.experimental.pallas import tpu as pltpu
from jax.sharding import PartitionSpec as P

ALPHA = 48.0**0.5
epsilon = 1e-05


def rotary(source):
    length = source.shape[0]
    half_dim = source.shape[-1] // 2
    frequency = 10000.0 ** (-2.0 * jnp.arange(half_dim, dtype=jnp.float32) / source.shape[-1])
    angles = jnp.arange(length, dtype=jnp.float32)[:, None] * frequency[None, :]
    cosine = jnp.cos(angles)[:, None, :]
    sine_table = jnp.sin(angles)[:, None, :]
    first_half = source[..., :half_dim]
    second = source[..., half_dim:]
    return jnp.concatenate(
        [first_half * cosine - second * sine_table, second * cosine + first_half * sine_table],
        axis=-1,
    )


def rope_pair(query_pre, key_pre):
    return (rotary(query_pre), rotary(key_pre))


def layer_norm(source, gain_vec, shift_vec):
    centred = source - jnp.mean(source, axis=-1, keepdims=True)
    variance = jnp.mean(centred * centred, axis=-1, keepdims=True)
    return centred * lax.rsqrt(variance + epsilon) * gain_vec + shift_vec


def geglu(gate_part, up_part):
    return jax.nn.gelu(gate_part) * up_part


def block_scores(query_block, key_bf, start, prefix_length, score_scale):
    length = key_bf.shape[0]
    scores = (
        jnp.einsum("qhd,khd->hqk", query_block, key_bf, preferred_element_type=jnp.float32)
        * score_scale
    )
    query_pos = start + jnp.arange(query_block.shape[0], dtype=jnp.int32)
    key_pos = jnp.arange(length, dtype=jnp.int32)
    visible = (key_pos[None, :] < prefix_length) | (key_pos[None, :] <= query_pos[:, None])
    return jnp.where(visible[None], scores, -1e30)


def shards(
    tokens,
    cotangent,
    loss_mask,
    prefix,
    counts,
    w_qkv,
    b_qkv,
    w_dense,
    b_dense,
    ln1_gain,
    ln1_bias,
    w_up,
    b_up,
    w_down,
    b_down,
    ln2_gain,
    ln2_bias,
):
    item_count = tokens.shape[1]
    row_count = tokens.shape[2]
    model_width = tokens.shape[3]
    length = row_count * lax.axis_size("tensor")
    local_heads = w_qkv.shape[1]
    head_dim = w_qkv.shape[2] // 3
    local_hidden = w_up.shape[2]
    block_rows = min(512, length)
    score_scale = head_dim ** (-0.5)
    group_id = lax.axis_index("obj")
    count_float = counts.astype(jnp.float32)
    share = jnp.where(group_id == 0, count_float[0], count_float[1]) / (
        count_float[0] + count_float[1]
    )
    bias_qkv = b_qkv.astype(jnp.float32)
    bias_dense = b_dense.astype(jnp.float32)
    gain_one = ln1_gain.astype(jnp.float32)
    shift_one = ln1_bias.astype(jnp.float32)
    bias_up = b_up.astype(jnp.float32)
    bias_down = b_down.astype(jnp.float32)
    gain_two = ln2_gain.astype(jnp.float32)
    shift_two = ln2_bias.astype(jnp.float32)

    def fetch():
        return (
            lax.all_gather(w_qkv, "dp", axis=0, tiled=True),
            lax.all_gather(w_dense, "dp", axis=2, tiled=True),
            lax.all_gather(w_up, "dp", axis=1, tiled=True),
            lax.all_gather(w_down, "dp", axis=1, tiled=True),
        )

    def one_item(item_slot, carry):
        outputs, grad_inputs, large_grads, bias_grads, norm_grads = carry
        qkv_full, dense_full, up_full, down_full = fetch()
        token_rows = lax.dynamic_index_in_dim(tokens[0], item_slot, 0, keepdims=False)
        prefix_length = jnp.where(group_id == 0, length, prefix[item_slot])
        gathered = lax.all_gather(token_rows, "tensor", axis=0, tiled=True)
        projected = (
            jnp.einsum("ld,dhe->lhe", gathered, qkv_full, preferred_element_type=jnp.float32)
            + bias_qkv
        )
        (query_rot, key_rot), rope_pull = jax.vjp(
            rope_pair, projected[..., :head_dim], projected[..., head_dim : 2 * head_dim]
        )
        query_bf = query_rot.astype(jnp.bfloat16)
        key_bf = key_rot.astype(jnp.bfloat16)
        value_bf = projected[..., 2 * head_dim :].astype(jnp.bfloat16)
        context_parts = []
        lse_parts = []
        for start in range(0, length, block_rows):
            scores = block_scores(
                query_bf[start : start + block_rows], key_bf, start, prefix_length, score_scale
            )
            highest_score = jnp.max(scores, axis=-1, keepdims=True)
            expo = jnp.exp(scores - highest_score)
            totals = jnp.sum(expo, axis=-1, keepdims=True)
            soft_weights = (expo / totals).astype(jnp.bfloat16)
            context_parts.append(
                jnp.einsum(
                    "hqk,khd->qhd", soft_weights, value_bf, preferred_element_type=jnp.float32
                )
            )
            lse_parts.append((highest_score + jnp.log(totals))[..., 0])
        context_bf = jnp.concatenate(context_parts, axis=0).astype(jnp.bfloat16)
        log_totals = jnp.concatenate(lse_parts, axis=1)
        source = token_rows.astype(jnp.float32)
        piece = lax.slice_in_dim(context_bf, 0, lax.axis_size("tensor") * row_count, axis=0)
        attn_rows = (
            lax.psum_scatter(
                jnp.einsum("lhd,hde->le", piece, dense_full, preferred_element_type=jnp.float32),
                "tensor",
                scatter_dimension=0,
                tiled=True,
            )
            + bias_dense
        )
        first_norm, norm_one_pull = jax.vjp(
            layer_norm, ALPHA * source + attn_rows, gain_one, shift_one
        )
        norm_full = lax.all_gather(first_norm.astype(jnp.bfloat16), "tensor", axis=0, tiled=True)
        gate_up = (
            jnp.einsum("ld,kdf->klf", norm_full, up_full, preferred_element_type=jnp.float32)
            + bias_up[:, None, :]
        )
        activated, act_pull = jax.vjp(geglu, gate_up[0], gate_up[1])
        hidden_bf = activated.astype(jnp.bfloat16)
        piece = lax.slice_in_dim(hidden_bf, 0, lax.axis_size("tensor") * row_count, axis=0)
        mlp_rows = (
            lax.psum_scatter(
                jnp.dot(piece, down_full, preferred_element_type=jnp.float32),
                "tensor",
                scatter_dimension=0,
                tiled=True,
            )
            + bias_down
        )
        result, norm_two_pull = jax.vjp(
            layer_norm, ALPHA * first_norm + mlp_rows, gain_two, shift_two
        )
        qkv_back, dense_back, up_back, down_back = fetch()
        mask_rows = lax.dynamic_index_in_dim(loss_mask[0], item_slot, 0, keepdims=False).astype(
            jnp.float32
        )
        cot_rows = lax.dynamic_index_in_dim(cotangent[0], item_slot, 0, keepdims=False).astype(
            jnp.float32
        )
        grad_out = cot_rows * mask_rows[:, None] * share
        grad_second, grad_gain_two, grad_shift_two = norm_two_pull(grad_out)
        grad_mlp = grad_second.astype(jnp.bfloat16)
        grad_bias_down = jnp.sum(grad_mlp.astype(jnp.float32), axis=0)
        grad_mlp_full = lax.all_gather(grad_mlp, "tensor", axis=0, tiled=True)
        grad_down = jnp.einsum(
            "lf,ld->fd", hidden_bf, grad_mlp_full, preferred_element_type=jnp.float32
        )
        grad_hidden = jnp.einsum(
            "ld,fd->lf", grad_mlp_full, down_back, preferred_element_type=jnp.float32
        )
        grad_gate, grad_upper = act_pull(grad_hidden)
        grad_gate_up = jnp.stack([grad_gate, grad_upper]).astype(jnp.bfloat16)
        grad_bias_up = jnp.sum(grad_gate_up.astype(jnp.float32), axis=1)
        grad_up = jnp.einsum(
            "ld,klf->kdf", norm_full, grad_gate_up, preferred_element_type=jnp.float32
        )
        piece = lax.slice_in_dim(grad_gate_up, 0, lax.axis_size("tensor") * row_count, axis=1)
        grad_norm_one = ALPHA * grad_second + lax.psum_scatter(
            jnp.einsum("klf,kdf->ld", piece, up_back, preferred_element_type=jnp.float32),
            "tensor",
            scatter_dimension=0,
            tiled=True,
        )
        grad_first, grad_gain_one, grad_shift_one = norm_one_pull(grad_norm_one)
        grad_attn = grad_first.astype(jnp.bfloat16)
        grad_bias_dense = jnp.sum(grad_attn.astype(jnp.float32), axis=0)
        grad_attn_full = lax.all_gather(grad_attn, "tensor", axis=0, tiled=True)
        grad_dense = jnp.einsum(
            "lhd,le->hde", context_bf, grad_attn_full, preferred_element_type=jnp.float32
        )
        grad_context = jnp.einsum(
            "le,hde->lhd", grad_attn_full, dense_back, preferred_element_type=jnp.float32
        ).astype(jnp.bfloat16)
        query_grads = []
        key_grad = jnp.zeros((length, local_heads, head_dim), jnp.float32)
        value_grad = jnp.zeros((length, local_heads, head_dim), jnp.float32)
        for start in range(0, length, block_rows):
            query_block = query_bf[start : start + block_rows]
            scores = block_scores(query_block, key_bf, start, prefix_length, score_scale)
            soft_full = jnp.exp(scores - log_totals[:, start : start + block_rows, None])
            context_block = grad_context[start : start + block_rows]
            grad_soft = jnp.einsum(
                "qhd,khd->hqk", context_block, value_bf, preferred_element_type=jnp.float32
            )
            grad_scores = (
                soft_full * (grad_soft - jnp.sum(soft_full * grad_soft, axis=-1, keepdims=True))
            ).astype(jnp.bfloat16)
            query_grads.append(
                jnp.einsum("hqk,khd->qhd", grad_scores, key_bf, preferred_element_type=jnp.float32)
                * score_scale
            )
            key_grad = (
                key_grad
                + jnp.einsum(
                    "hqk,qhd->khd", grad_scores, query_block, preferred_element_type=jnp.float32
                )
                * score_scale
            )
            value_grad = value_grad + jnp.einsum(
                "hqk,qhd->khd",
                soft_full.astype(jnp.bfloat16),
                context_block,
                preferred_element_type=jnp.float32,
            )
        grad_query_pre, grad_key_pre = rope_pull((jnp.concatenate(query_grads, axis=0), key_grad))
        grad_projected = jnp.concatenate(
            [grad_query_pre, grad_key_pre, value_grad], axis=-1
        ).astype(jnp.bfloat16)
        grad_bias_qkv = jnp.sum(grad_projected.astype(jnp.float32), axis=0)
        grad_qkv = jnp.einsum(
            "ld,lhe->dhe", gathered, grad_projected, preferred_element_type=jnp.float32
        )
        piece = lax.slice_in_dim(grad_projected, 0, row_count * lax.axis_size("tensor"), axis=0)
        grad_source = ALPHA * grad_first + lax.psum_scatter(
            jnp.einsum("lhe,dhe->ld", piece, qkv_back, preferred_element_type=jnp.float32).astype(
                jnp.bfloat16
            ),
            "tensor",
            scatter_dimension=0,
            tiled=True,
        ).astype(jnp.float32)
        outputs = lax.dynamic_update_index_in_dim(
            outputs, result.astype(jnp.bfloat16), item_slot, 0
        )
        grad_inputs = lax.dynamic_update_index_in_dim(grad_inputs, grad_source, item_slot, 0)
        large_grads = (
            large_grads[0] + grad_qkv,
            large_grads[1] + grad_dense,
            large_grads[2] + grad_up,
            large_grads[3] + grad_down,
        )
        bias_grads = (bias_grads[0] + grad_bias_qkv, bias_grads[1] + grad_bias_up)
        norm_grads = (
            norm_grads[0] + grad_bias_dense,
            norm_grads[1] + grad_gain_one,
            norm_grads[2] + grad_shift_one,
            norm_grads[3] + grad_bias_down,
            norm_grads[4] + grad_gain_two,
            norm_grads[5] + grad_shift_two,
        )
        return (outputs, grad_inputs, large_grads, bias_grads, norm_grads)

    zero_vector = jnp.zeros((model_width,), jnp.float32)
    initial = (
        jnp.zeros((item_count, row_count, model_width), jnp.bfloat16),
        jnp.zeros((item_count, row_count, model_width), jnp.float32),
        (
            jnp.zeros((model_width, local_heads, 3 * head_dim), jnp.float32),
            jnp.zeros((local_heads, head_dim, model_width), jnp.float32),
            jnp.zeros((2, model_width, local_hidden), jnp.float32),
            jnp.zeros((local_hidden, model_width), jnp.float32),
        ),
        (
            jnp.zeros((local_heads, 3 * head_dim), jnp.float32),
            jnp.zeros((2, local_hidden), jnp.float32),
        ),
        (zero_vector, zero_vector, zero_vector, zero_vector, zero_vector, zero_vector),
    )
    outputs, grad_inputs, large_grads, bias_grads, norm_grads = lax.fori_loop(
        0, item_count, one_item, initial
    )
    sharded = (
        lax.psum_scatter(
            large_grads[0].astype(jnp.bfloat16), "dp", scatter_dimension=0, tiled=True
        ).astype(jnp.float32),
        lax.psum_scatter(
            large_grads[1].astype(jnp.bfloat16), "dp", scatter_dimension=2, tiled=True
        ).astype(jnp.float32),
        lax.psum_scatter(
            large_grads[2].astype(jnp.bfloat16), "dp", scatter_dimension=1, tiled=True
        ).astype(jnp.float32),
        lax.psum_scatter(
            large_grads[3].astype(jnp.bfloat16), "dp", scatter_dimension=1, tiled=True
        ).astype(jnp.float32),
    )
    merged = (
        lax.psum(sharded[0].astype(jnp.bfloat16), "obj").astype(jnp.float32),
        lax.psum(sharded[1].astype(jnp.bfloat16), "obj").astype(jnp.float32),
        lax.psum(sharded[2].astype(jnp.bfloat16), "obj").astype(jnp.float32),
        lax.psum(sharded[3].astype(jnp.bfloat16), "obj").astype(jnp.float32),
    )
    bias_total = lax.psum((bias_grads[0], bias_grads[1]), ("obj", "dp"))
    norm_total = lax.psum(
        (norm_grads[0], norm_grads[1], norm_grads[2], norm_grads[3], norm_grads[4], norm_grads[5]),
        ("obj", "dp", "tensor"),
    )
    return (
        outputs[None],
        grad_inputs[None],
        merged[0],
        bias_total[0],
        merged[1],
        norm_total[0],
        norm_total[1],
        norm_total[2],
        merged[2],
        bias_total[1],
        merged[3],
        norm_total[3],
        norm_total[4],
        norm_total[5],
    )


def paced(flops):
    return pl.CostEstimate(flops=int(flops / 2), bytes_accessed=1, transcendentals=0)


def attend(projected, cos_table, sin_table, key_pos, query_pos, limit, first, heads, head_dim):
    length = projected.shape[0]
    block = min(256, length)
    score_scale = head_dim ** (-0.5)
    half_dim = head_dim // 2

    def kernel(limit_ref, proj_ref, cos_ref, sin_ref, kpos_ref, qpos_ref, ctx_ref, qkv_ref, lse_ref):
        cosine = cos_ref[...]
        sine = sin_ref[...]
        query = proj_ref[:, :head_dim].astype(jnp.float32)
        key = proj_ref[:, head_dim : 2 * head_dim].astype(jnp.float32)
        query = query * cosine + pltpu.roll(query, half_dim, 1) * sine
        key = key * cosine + pltpu.roll(key, half_dim, 1) * sine
        qkv_ref[:, :head_dim] = query.astype(jnp.bfloat16)
        key_bf = key.astype(jnp.bfloat16)
        qkv_ref[:, head_dim : 2 * head_dim] = key_bf
        value_bf = proj_ref[:, 2 * head_dim :].astype(jnp.bfloat16)
        qkv_ref[:, 2 * head_dim :] = value_bf
        prefix_length = limit_ref[0]
        near = kpos_ref[...] < prefix_length
        for start in range(0, length, block):
            rows = slice(start, start + block)
            scores = (
                lax.dot_general(
                    key_bf,
                    qkv_ref[rows, :head_dim],
                    (((1,), (1,)), ((), ())),
                    preferred_element_type=jnp.float32,
                )
                * score_scale
            )
            visible = near | (kpos_ref[...] <= qpos_ref[:, rows])
            scores = jnp.where(visible, scores, -1e30)
            highest_score = jnp.max(scores, axis=0, keepdims=True)
            expo = jnp.exp(scores - highest_score)
            totals = jnp.sum(expo, axis=0, keepdims=True)
            weights = (expo / totals).astype(jnp.bfloat16)
            ctx_ref[rows, :] = lax.dot_general(
                weights,
                value_bf,
                (((0,), (0,)), ((), ())),
                preferred_element_type=jnp.float32,
            ).astype(jnp.bfloat16)
            lse_ref[0, :, rows] = highest_score + jnp.log(totals)

    fixed = lambda h, lim: (0, 0)
    return pl.pallas_call(
        kernel,
        grid_spec=pltpu.PrefetchScalarGridSpec(
            num_scalar_prefetch=1,
            grid=(heads,),
            in_specs=[
                pl.BlockSpec((length, 3 * head_dim), lambda h, lim: (0, h + first)),
                pl.BlockSpec((length, head_dim), fixed),
                pl.BlockSpec((length, head_dim), fixed),
                pl.BlockSpec((length, 1), fixed),
                pl.BlockSpec((1, length), fixed),
            ],
            out_specs=[
                pl.BlockSpec((length, head_dim), lambda h, lim: (0, h)),
                pl.BlockSpec((length, 3 * head_dim), lambda h, lim: (0, h)),
                pl.BlockSpec((1, 1, length), lambda h, lim: (h, 0, 0)),
            ],
        ),
        out_shape=[
            jax.ShapeDtypeStruct((length, heads * head_dim), jnp.bfloat16),
            jax.ShapeDtypeStruct((length, heads * 3 * head_dim), jnp.bfloat16),
            jax.ShapeDtypeStruct((heads, 1, length), jnp.float32),
        ],
        compiler_params=pltpu.CompilerParams(vmem_limit_bytes=48 * 1024 * 1024),
        cost_estimate=paced(8 * heads * length * length * head_dim),
        name="attend",
    )(limit, projected, cos_table, sin_table, key_pos, query_pos)


def attend_back(
    grad_context,
    qkv,
    log_totals,
    cos_table,
    sin_table,
    key_pos,
    query_pos,
    limit,
    first,
    heads,
    head_dim,
):
    length = qkv.shape[0]
    block = min(256, length)
    score_scale = head_dim ** (-0.5)
    half_dim = head_dim // 2

    def kernel(
        limit_ref,
        qkv_ref,
        grad_ref,
        lse_ref,
        cos_ref,
        sin_ref,
        kpos_ref,
        qpos_ref,
        out_ref,
        bias_ref,
        query_grad,
        key_grad,
        value_grad,
    ):
        key_bf = qkv_ref[:, head_dim : 2 * head_dim]
        value_bf = qkv_ref[:, 2 * head_dim :]
        prefix_length = limit_ref[0]
        near = kpos_ref[...] < prefix_length
        for start in range(0, length, block):
            rows = slice(start, start + block)
            query_block = qkv_ref[rows, :head_dim]
            grad_block = grad_ref[rows, :]
            scores = (
                lax.dot_general(
                    key_bf,
                    query_block,
                    (((1,), (1,)), ((), ())),
                    preferred_element_type=jnp.float32,
                )
                * score_scale
            )
            visible = near | (kpos_ref[...] <= qpos_ref[:, rows])
            soft = jnp.exp(jnp.where(visible, scores, -1e30) - lse_ref[0, :, rows])
            grad_soft = lax.dot_general(
                value_bf,
                grad_block,
                (((1,), (1,)), ((), ())),
                preferred_element_type=jnp.float32,
            )
            inner = jnp.sum(soft * grad_soft, axis=0, keepdims=True)
            grad_scores = (soft * (grad_soft - inner)).astype(jnp.bfloat16)
            query_grad[rows, :] = (
                lax.dot_general(
                    grad_scores,
                    key_bf,
                    (((0,), (0,)), ((), ())),
                    preferred_element_type=jnp.float32,
                )
                * score_scale
            )
            key_term = (
                jnp.dot(grad_scores, query_block, preferred_element_type=jnp.float32) * score_scale
            )
            value_term = jnp.dot(
                soft.astype(jnp.bfloat16), grad_block, preferred_element_type=jnp.float32
            )
            if start == 0:
                key_grad[...] = key_term
                value_grad[...] = value_term
            else:
                key_grad[...] += key_term
                value_grad[...] += value_term
        cosine = cos_ref[...]
        sine = sin_ref[...]
        turned = query_grad[...]
        turned = (turned * cosine + pltpu.roll(turned * sine, half_dim, 1)).astype(jnp.bfloat16)
        out_ref[:, :head_dim] = turned
        bias_ref[0, :, :head_dim] = jnp.sum(turned.astype(jnp.float32), axis=0, keepdims=True)
        turned = key_grad[...]
        turned = (turned * cosine + pltpu.roll(turned * sine, half_dim, 1)).astype(jnp.bfloat16)
        out_ref[:, head_dim : 2 * head_dim] = turned
        bias_ref[0, :, head_dim : 2 * head_dim] = jnp.sum(
            turned.astype(jnp.float32), axis=0, keepdims=True
        )
        turned = value_grad[...].astype(jnp.bfloat16)
        out_ref[:, 2 * head_dim :] = turned
        bias_ref[0, :, 2 * head_dim :] = jnp.sum(turned.astype(jnp.float32), axis=0, keepdims=True)

    fixed = lambda h, lim: (0, 0)
    return pl.pallas_call(
        kernel,
        grid_spec=pltpu.PrefetchScalarGridSpec(
            num_scalar_prefetch=1,
            grid=(heads,),
            in_specs=[
                pl.BlockSpec((length, 3 * head_dim), lambda h, lim: (0, h)),
                pl.BlockSpec((length, head_dim), lambda h, lim: (0, h + first)),
                pl.BlockSpec((1, 1, length), lambda h, lim: (h, 0, 0)),
                pl.BlockSpec((length, head_dim), fixed),
                pl.BlockSpec((length, head_dim), fixed),
                pl.BlockSpec((length, 1), fixed),
                pl.BlockSpec((1, length), fixed),
            ],
            out_specs=[
                pl.BlockSpec((length, 3 * head_dim), lambda h, lim: (0, h)),
                pl.BlockSpec((1, 1, 3 * head_dim), lambda h, lim: (h, 0, 0)),
            ],
            scratch_shapes=[pltpu.VMEM((length, head_dim), jnp.float32)] * 3,
        ),
        out_shape=[
            jax.ShapeDtypeStruct((length, heads * 3 * head_dim), jnp.bfloat16),
            jax.ShapeDtypeStruct((heads, 1, 3 * head_dim), jnp.float32),
        ],
        compiler_params=pltpu.CompilerParams(vmem_limit_bytes=48 * 1024 * 1024),
        cost_estimate=paced(10 * heads * length * length * head_dim),
        name="attend_back",
    )(limit, qkv, grad_context, log_totals, cos_table, sin_table, key_pos, query_pos)


def transposed_dot(left, right):
    return lax.dot_general(
        left, right, (((1,), (1,)), ((), ())), preferred_element_type=jnp.float32
    )


def rows_outer(features, right):
    return lax.dot_general(
        features, right, (((0,), (0,)), ((), ())), preferred_element_type=jnp.float32
    )


VMEM_BYTES = 60 * 1024 * 1024


def join(parts, count, target, total, offset):
    width = parts[0][0].shape[1]
    rows = count
    while offset % rows or any(first % rows for _, first in parts):
        rows //= 2
    steps = count // rows

    def kernel(*refs):
        for index in range(4):

            @pl.when(pl.program_id(1) == index)
            def _():
                refs[-1][...] = refs[index][...]

    def source(first):
        return pl.BlockSpec((rows, width), lambda i, p: (first // rows + i, 0))

    given = [] if target is None else [target]
    return pl.pallas_call(
        kernel,
        grid=(steps, 4),
        in_specs=[source(first) for _, first in parts]
        + [pl.BlockSpec(memory_space=pl.ANY)] * len(given),
        out_specs=pl.BlockSpec((rows, width), lambda i, p: (offset // rows + p * steps + i, 0)),
        out_shape=jax.ShapeDtypeStruct((total, width), parts[0][0].dtype),
        input_output_aliases={4: 0} if given else {},
        compiler_params=pltpu.CompilerParams(vmem_limit_bytes=VMEM_BYTES),
        cost_estimate=paced(1000 * count * width),
        name="join",
    )(*[array for array, _ in parts], *given)


def pack(arrays):
    total = sum(array.shape[0] for array in arrays)

    def kernel(*refs):
        row = 0
        for ref in refs[:-1]:
            refs[-1][row : row + ref.shape[0]] = ref[...]
            row += ref.shape[0]

    return pl.pallas_call(
        kernel,
        out_shape=jax.ShapeDtypeStruct((total, 128), arrays[0].dtype),
        cost_estimate=paced(1),
        name="pack",
    )(*arrays)


def block_of(count, sizes=(512, 256, 128)):
    for size in sizes:
        if count % size == 0:
            return size
    return count


class Weight:
    def __init__(self, arrays, start, count):
        self.arrays = arrays
        self.start = start
        self.count = count
        self.part = arrays[0].shape[1]
        self.width = 4 * self.part

    def row_specs(self, block):
        return [pl.BlockSpec((block, self.part), lambda j: (self.start // block + j, 0))] * 4


def project_block(rows_ref, weight_refs):
    total = None
    for index, ref in enumerate(weight_refs):
        part = ref.shape[1]
        product = transposed_dot(rows_ref[:, index * part : (index + 1) * part], ref[...])
        total = product if total is None else total + product
    return total


def project(rows, weight, bias, kind):
    count, width = rows.shape
    features = weight.count
    block = block_of(features)

    def kernel(rows_ref, w0, w1, w2, w3, bias_ref, out_ref):
        result = project_block(rows_ref, (w0, w1, w2, w3))
        out_ref[...] = (result + bias_ref[...]).astype(kind)

    return pl.pallas_call(
        kernel,
        grid=(features // block,),
        in_specs=[pl.BlockSpec((count, width), lambda j: (0, 0))]
        + weight.row_specs(block)
        + [pl.BlockSpec((1, block), lambda j: (0, j))],
        out_specs=pl.BlockSpec((count, block), lambda j: (0, j)),
        out_shape=jax.ShapeDtypeStruct((count, features), kind),
        compiler_params=pltpu.CompilerParams(vmem_limit_bytes=VMEM_BYTES),
        cost_estimate=paced(2 * count * width * features),
        name="project",
    )(rows, *weight.arrays, bias)


def ff_forward(rows, gate_weight, upper_weight, bias_gate, bias_upper):
    count, width = rows.shape
    features = gate_weight.count
    block = block_of(features)

    def kernel(rows_ref, *refs):
        bg_ref, bu_ref, gate_ref, upper_ref, hid_ref = refs[8:]
        gate = project_block(rows_ref, refs[:4]) + bg_ref[...]
        upper = project_block(rows_ref, refs[4:8]) + bu_ref[...]
        gate_ref[...] = gate.astype(jnp.bfloat16)
        upper_ref[...] = upper.astype(jnp.bfloat16)
        hid_ref[...] = (jax.nn.gelu(gate) * upper).astype(jnp.bfloat16)

    out = jax.ShapeDtypeStruct((count, features), jnp.bfloat16)
    return pl.pallas_call(
        kernel,
        grid=(features // block,),
        in_specs=[pl.BlockSpec((count, width), lambda j: (0, 0))]
        + gate_weight.row_specs(block)
        + upper_weight.row_specs(block)
        + [pl.BlockSpec((1, block), lambda j: (0, j))] * 2,
        out_specs=[pl.BlockSpec((count, block), lambda j: (0, j))] * 3,
        out_shape=[out, out, out],
        compiler_params=pltpu.CompilerParams(vmem_limit_bytes=VMEM_BYTES),
        cost_estimate=paced(4 * count * width * features),
        name="ff_forward",
    )(rows, *gate_weight.arrays, *upper_weight.arrays, bias_gate, bias_upper)


def ff_back(rows, down_weight, gate, upper):
    count, width = rows.shape
    features = down_weight.count
    block = block_of(features)
    factor = (2.0 / math.pi) ** 0.5

    def kernel(rows_ref, w0, w1, w2, w3, gate_ref, upper_ref, gg_ref, gu_ref, sg_ref, su_ref):
        grad = project_block(rows_ref, (w0, w1, w2, w3))
        value = gate_ref[...].astype(jnp.float32)
        square = value * value
        bend = jnp.tanh(factor * value * (1.0 + 0.044715 * square))
        lift = 0.5 * (1.0 + bend)
        slope = lift + 0.5 * value * (1.0 - bend * bend) * (
            factor * (1.0 + 3.0 * 0.044715 * square)
        )
        grad_gate = (grad * upper_ref[...].astype(jnp.float32) * slope).astype(jnp.bfloat16)
        grad_upper = (grad * (value * lift)).astype(jnp.bfloat16)
        gg_ref[...] = grad_gate
        gu_ref[...] = grad_upper
        sg_ref[...] = jnp.sum(grad_gate.astype(jnp.float32), axis=0, keepdims=True)
        su_ref[...] = jnp.sum(grad_upper.astype(jnp.float32), axis=0, keepdims=True)

    out = jax.ShapeDtypeStruct((count, features), jnp.bfloat16)
    row = jax.ShapeDtypeStruct((1, features), jnp.float32)
    return pl.pallas_call(
        kernel,
        grid=(features // block,),
        in_specs=[pl.BlockSpec((count, width), lambda j: (0, 0))]
        + down_weight.row_specs(block)
        + [pl.BlockSpec((count, block), lambda j: (0, j))] * 2,
        out_specs=[pl.BlockSpec((count, block), lambda j: (0, j))] * 2
        + [pl.BlockSpec((1, block), lambda j: (0, j))] * 2,
        out_shape=[out, out, row, row],
        compiler_params=pltpu.CompilerParams(vmem_limit_bytes=VMEM_BYTES),
        cost_estimate=paced(3 * count * width * features),
        name="ff_back",
    )(rows, *down_weight.arrays, gate, upper)


def expand(*pairs):
    count = pairs[0][0].shape[0]
    width = pairs[0][1].width
    part = width // 4
    own = count // 2
    terms = len(pairs)
    cuts = 2 if sum(weight.count for _, weight in pairs) > 4000 else 1
    block = part // cuts

    def kernel(*refs):
        own_ref, other_ref = refs[5 * terms :]
        for which in range(4):

            @pl.when(pl.program_id(0) // cuts == which)
            def _():
                total = None
                for term in range(terms):
                    product = jnp.dot(
                        refs[5 * term][...],
                        refs[5 * term + 1 + which][...],
                        preferred_element_type=jnp.float32,
                    )
                    total = product if total is None else total + product
                own_ref[...] = total[:own]
                other_ref[...] = total[own:].astype(jnp.bfloat16)

    def column(weight, which):
        return pl.BlockSpec(
            (weight.count, block),
            lambda j: (weight.start // weight.count, jnp.clip(j - cuts * which, 0, cuts - 1)),
        )

    specs = []
    operands = []
    for features, weight in pairs:
        specs.append(pl.BlockSpec((count, weight.count), lambda j: (0, 0)))
        specs += [column(weight, which) for which in range(4)]
        operands += [features, *weight.arrays]
    return pl.pallas_call(
        kernel,
        grid=(4 * cuts,),
        in_specs=specs,
        out_specs=[pl.BlockSpec((own, block), lambda j: (0, j))] * 2,
        out_shape=[
            jax.ShapeDtypeStruct((own, width), jnp.float32),
            jax.ShapeDtypeStruct((own, width), jnp.bfloat16),
        ],
        compiler_params=pltpu.CompilerParams(vmem_limit_bytes=VMEM_BYTES),
        cost_estimate=paced(2 * count * width * sum(weight.count for _, weight in pairs)),
        name="expand",
    )(*operands)


def outer(features, rights, start, columns, parts, added=(), pieces=(), steps=2):
    chunks = len(features)
    count = rights[0][2]
    total = features[0][0].shape[1]
    block = total // steps
    rows = total // parts

    def kernel(*refs):
        result = None
        for chunk in range(chunks):
            product = rows_outer(refs[chunk][...], refs[chunks + chunk][...])
            result = product if result is None else result + product
        first = 2 * chunks
        for ref in refs[first : first + len(added)]:
            result = result + ref[...].astype(jnp.float32)
        first += len(added)
        outs = refs[first + len(pieces) :]
        if parts == 1:
            outs[0][...] = result.astype(jnp.bfloat16)
            return
        each = parts // steps
        for half in range(steps):

            @pl.when(pl.program_id(0) == half)
            def _():
                whole = result
                if pieces:
                    whole = whole + refs[first + half][...].astype(jnp.float32)
                whole = whole.astype(jnp.bfloat16)
                for index in range(each):
                    outs[half * each + index][...] = whole[index * rows : (index + 1) * rows]

    def at(row, column):
        return lambda j: (row, column)

    def across(row):
        return lambda j: (row, j)

    def along(column):
        return lambda j: (j, column)

    if parts == 1:
        out_specs = [pl.BlockSpec((block, columns), along(0))]
    else:
        out_specs = [pl.BlockSpec((rows, columns), at(0, 0))] * parts
    return pl.pallas_call(
        kernel,
        grid=(steps,),
        in_specs=[pl.BlockSpec((count, block), across(row)) for _, row, _ in features]
        + [pl.BlockSpec((count, columns), at(row, start // columns)) for _, row, _ in rights]
        + [pl.BlockSpec((block, columns), along(column // columns)) for _, column in added]
        + [pl.BlockSpec((block, columns), at(0, 0))] * len(pieces),
        out_specs=out_specs,
        out_shape=[jax.ShapeDtypeStruct((rows, columns), jnp.bfloat16)] * parts,
        compiler_params=pltpu.CompilerParams(vmem_limit_bytes=VMEM_BYTES),
        cost_estimate=paced(3 * chunks * count * total * columns),
        name="outer",
    )(
        *[array for array, _, _ in features],
        *[array for array, _, _ in rights],
        *[array for array, _ in added],
        *pieces,
    )


def after(values, *earlier):
    return lax.optimization_barrier((values,) + earlier)[0]


CHUNKS = 2


def pair_shards(
    tokens,
    cotangent,
    loss_mask,
    prefix,
    counts,
    w_qkv,
    b_qkv,
    w_dense,
    b_dense,
    ln1_gain,
    ln1_bias,
    w_up,
    b_up,
    w_down,
    b_down,
    ln2_gain,
    ln2_bias,
):
    slots, home_rows, width = tokens.shape[1:]
    n_tensor = lax.axis_size("tensor")
    length = home_rows * n_tensor
    own_count = length // 2
    head_dim = w_qkv.shape[2] // 3
    shard_heads = w_qkv.shape[1]
    heads = 2 * shard_heads
    shard_hidden = w_up.shape[2]
    block_width = w_qkv.shape[0]
    side = lax.axis_index("obj")
    place = lax.axis_index("dp")
    layer = lax.axis_index("tensor")
    item_slot = layer >> 1

    def along(axis, step, depth=2):
        moves = [(i, i ^ step) for i in range(lax.axis_size(axis))]
        sent = []

        def move(values):
            if len(sent) >= depth:
                values = after(values, sent[-depth])
            sent.append(lax.ppermute(values, axis, moves))
            return sent[-1]

        return move

    over_x = along("obj", 1)
    over_y = along("dp", 2)
    over_core = along("dp", 1)
    swap = along("tensor", 1, 1)
    over_far = along("tensor", 2, 1)
    back_x = along("obj", 1, 2)
    back_y = along("dp", 2, 2)
    back_far = along("tensor", 2, 1)

    def to_local(values):
        parts = [
            lax.dynamic_slice_in_dim(values, (place ^ k) * block_width, block_width, -1)
            for k in (0, 2, 1, 3)
        ]
        return jnp.concatenate(parts, axis=-1)

    def from_local(values):
        parts = []
        for g in range(4):
            k = place ^ g
            at = ((k & 1) << 1) | (k >> 1)
            parts.append(lax.dynamic_slice_in_dim(values, at * block_width, block_width, -1))
        return jnp.concatenate(parts, axis=-1)

    def away(values):
        stays = lax.dynamic_index_in_dim(values, item_slot, 0, keepdims=False)
        leaves = lax.dynamic_index_in_dim(values, 1 - item_slot, 0, keepdims=False)
        return [stays, over_far(leaves)]

    def home(values):
        stays, leaves = values
        came = back_far(leaves)
        first = jnp.where(item_slot == 0, stays, came)
        second = jnp.where(item_slot == 0, came, stays)
        return from_local(jnp.stack([first, second])), came

    def side_first(values, axis=0):
        count = values.shape[axis] // 2
        return (
            lax.dynamic_slice_in_dim(values, side * count, count, axis),
            lax.dynamic_slice_in_dim(values, (1 - side) * count, count, axis),
        )

    def sides(mine, other):
        return jnp.concatenate(
            [jnp.where(side == 0, mine, other), jnp.where(side == 0, other, mine)], axis=0
        )

    latest = []

    def turn(work, first, *rest, wait=()):
        result = work(after(first, *latest, *wait), *rest)
        latest[:] = [result[0] if isinstance(result, (tuple, list)) else result]
        return result

    narrow = jnp.bfloat16
    wide = jnp.float32

    class Gathering:
        def __init__(self, *shards):
            halves = [side_first(shard) for shard in shards]
            self.mine = jnp.concatenate([half[0] for half in halves], axis=0)
            self.rest = jnp.concatenate([half[1] for half in halves], axis=0)
            self.counts = [half[0].shape[0] for half in halves]

        def to_far(self):
            self.far = over_far(self.mine)

        def far_to_y(self):
            self.far_y = over_y(self.far)

        def far_to_x(self):
            self.other_far = over_x(self.far)

        def both_to_x(self):
            self.other_far_y = over_x(self.far_y)

        def joined(self, parts, wait):
            total = 4 * sum(self.counts)
            target = None
            first = 0
            for count in self.counts:
                rest = [(array, start + first) for array, start in parts[1:]]
                target = turn(
                    lambda array: join(
                        [(array, parts[0][1] + first)] + rest, count, target, total, 4 * first
                    ),
                    parts[0][0],
                    wait=wait,
                )
                first += count
            return target

        def blocks(self, wait=()):
            near = self.joined(
                [(self.mine, 0), (self.rest, 0), (self.far, 0), (self.other_far, 0)], wait
            )
            next_y = self.joined(
                [self.near_y, self.other_y, (self.far_y, 0), (self.other_far_y, 0)], ()
            )
            self.near = near, over_core(near)
            self.next = next_y, over_core(next_y)

        def weights(self):
            arrays = (self.near[0], self.next[0], self.near[1], self.next[1])
            first = 0
            result = []
            for count in self.counts:
                result.append(Weight(arrays, 4 * first, 4 * count))
                first += count
            return result

    class Reduction:
        def __init__(self, features, rights):
            self.features = features
            self.rights = rights

        def part(self, *given, wait=(), **more):
            array, row, count = self.features[0]
            return turn(
                lambda first: outer(
                    [(first, row, count)] + self.features[1:], self.rights, *given, **more
                ),
                array,
                wait=wait,
            )

        def to_core(self, wait=()):
            (sent,) = self.part(2 * block_width, 2 * block_width, 1, wait=wait)
            self.came = over_core(sent)

        def to_y(self, wait=()):
            sent = self.part(
                block_width, block_width, 2, added=[(self.came, block_width)], wait=wait
            )
            far = back_y(sent[1])
            self.came_y = [back_y(sent[0]), far]

        def to_x(self, wait=()):
            near, near_sent, far, far_sent = self.part(
                0, block_width, 4, added=[(self.came, 0)], pieces=self.came_y, wait=wait
            )
            self.far = (far, back_x(far_sent))
            self.near = (near, back_x(near_sent))

        def to_x_first(self, wait=()):
            near, near_sent, far, far_sent = self.part(
                0, 2 * block_width, 4, added=[(self.came, 0)], wait=wait
            )
            self.wide_far = (far, back_x(far_sent))
            self.wide_near = (near, back_x(near_sent))

        def to_y_next(self):
            def onward(pair):
                summed = add(*pair)
                return summed[:, :block_width], back_y(summed[:, block_width:])

            self.far = onward(self.wide_far)
            self.near = onward(self.wide_near)

        def to_far(self):
            self.came_far = back_far(add(*self.far))

        def finish(self):
            self.mine = add(*self.near, self.came_far)
            return sides(self.mine, back_x(self.mine)).astype(wide)

    class HalfReduction:
        def __init__(self, features, rights):
            self.features = features
            self.rights = rights

        def part(self, *given, wait=(), **more):
            array, row, count = self.features[0]
            return turn(
                lambda first: outer(
                    [(first, row, count)] + self.features[1:],
                    self.rights,
                    *given,
                    steps=1,
                    **more,
                ),
                array,
                wait=wait,
            )

        def to_core(self, wait=()):
            (sent,) = self.part(2 * block_width, 2 * block_width, 1, wait=wait)
            self.came = over_core(sent)

        def to_y(self, wait=()):
            (sent,) = self.part(
                block_width, block_width, 1, added=[(self.came, block_width)], wait=wait
            )
            self.came_y = back_y(sent)

        def to_x(self, wait=()):
            kept, sent = self.part(
                0, block_width, 2, added=[(self.came, 0), (self.came_y, 0)], wait=wait
            )
            self.pair = (kept, back_x(sent))

    def add(*values):
        total = values[0].astype(wide)
        for value in values[1:]:
            total = total + value.astype(wide)
        return total.astype(narrow)

    count_float = counts.astype(jnp.float32)
    share = jnp.where(side == 0, count_float[0], count_float[1]) / (
        count_float[0] + count_float[1]
    )
    limit = jnp.where(side == 0, length, prefix[item_slot]).astype(jnp.int32).reshape(1)

    shard_qkv = w_qkv.reshape(block_width, shard_heads * 3 * head_dim).T
    shard_dense = w_dense.reshape(shard_heads * head_dim, block_width)
    up_rows = jnp.swapaxes(w_up, 1, 2)

    near_bias = jnp.concatenate(
        side_first(b_qkv.reshape(-1))
        + side_first(b_up[0])
        + side_first(b_up[1])
    )
    far_bias = lax.ppermute(near_bias, "tensor", [(i, i ^ 2) for i in range(n_tensor)])
    n_qkv = b_qkv.size

    def bias_row(start, count):
        parts = [near_bias[start : start + count], far_bias[start : start + count]]
        return jnp.concatenate(parts).astype(jnp.float32)[None]

    bias_qkv = bias_row(0, n_qkv)
    bias_gate = bias_row(n_qkv, shard_hidden)
    bias_upper = bias_row(n_qkv + shard_hidden, shard_hidden)

    def row_vector(values):
        return to_local(values.astype(jnp.float32)[None])

    bias_dense = row_vector(b_dense)
    gain_one = row_vector(ln1_gain)
    shift_one = row_vector(ln1_bias)
    bias_down = row_vector(b_down)
    gain_two = row_vector(ln2_gain)
    shift_two = row_vector(ln2_bias)

    share_rows = own_count // CHUNKS

    def positions(owner):
        return owner * home_rows + jnp.arange(home_rows, dtype=jnp.int32)

    where_rows = jnp.concatenate([positions(layer ^ k) for k in (0, 1, 2, 3)])
    key_pos = where_rows[:, None]
    query_pos = where_rows[None, :]
    half_dim = head_dim // 2
    frequency = 10000.0 ** (-2.0 * jnp.arange(half_dim, dtype=jnp.float32) / head_dim)
    angles = where_rows.astype(jnp.float32)[:, None] * frequency[None, :]
    cos_table = jnp.cos(angles)
    cos_table = jnp.concatenate([cos_table, cos_table], axis=1)
    sin_table = jnp.sin(angles)
    sin_table = jnp.concatenate([-sin_table, sin_table], axis=1)

    masked = cotangent[0] * loss_mask[0].astype(jnp.bfloat16)[..., None]
    early = Gathering(shard_qkv, shard_dense)
    middle = Gathering(up_rows[0])
    third = Gathering(up_rows[1])
    late = Gathering(w_down)

    early.to_far()
    early_y = over_y(early.mine)
    leaving = to_local(tokens[0])
    stays = lax.dynamic_index_in_dim(leaving, item_slot, 0, keepdims=False)
    came_tokens = [swap(stays)]
    others = (middle, third, late)
    others_y = over_y(jnp.concatenate([part.mine for part in others], axis=0))
    early_other_y = over_x(early_y)
    early.near_y = early_y, 0
    early.other_y = early_other_y, 0
    early.far = after(early.far, came_tokens[0], early_other_y)
    own_tokens = away(leaving)
    early.far_to_y()
    early.far_to_x()
    middle.to_far()
    early.both_to_x()
    early.blocks(wait=(own_tokens[1],))
    came_tokens.append(swap(own_tokens[1]))
    others_other_y = over_x(others_y)
    first_row = 0
    for part in others:
        part.near_y = others_y, first_row
        part.other_y = others_other_y, first_row
        first_row += part.counts[0]
    third.to_far()
    full_qkv, full_dense = early.weights()
    token_rows = jnp.concatenate(
        [part for i in range(CHUNKS) for part in (own_tokens[i], came_tokens[i])], axis=0
    )
    projected = turn(project, token_rows, full_qkv, bias_qkv, jnp.float32)

    def attend_heads(first, wait):
        return turn(
            attend,
            projected,
            cos_table,
            sin_table,
            key_pos,
            query_pos,
            limit,
            first,
            shard_heads,
            head_dim,
            wait=wait,
        )

    middle.far_to_y()
    middle.far_to_x()
    near_heads = attend_heads(0, (others_other_y,))
    late.to_far()
    far_heads = attend_heads(shard_heads, (middle.far_y, middle.other_far))
    middle.both_to_x()
    third.far_to_y()
    third.far_to_x()

    step = 2 * share_rows
    half_heads = shard_heads * head_dim
    dense_near = Weight(full_dense.arrays, full_dense.start, half_heads)
    dense_far = Weight(full_dense.arrays, full_dense.start + half_heads, half_heads)
    states = [dict() for _ in range(CHUNKS)]

    def normalize(values):
        centred = values - jnp.mean(values, axis=-1, keepdims=True)
        scale = lax.rsqrt(jnp.mean(centred * centred, axis=-1, keepdims=True) + epsilon)
        return centred * scale, scale

    def normalize_back(grad, gain, normal, scale):
        turned = grad * gain
        return scale * (
            turned
            - jnp.mean(turned, axis=-1, keepdims=True)
            - normal * jnp.mean(turned * normal, axis=-1, keepdims=True)
        )

    for i, state in enumerate(states):
        rows = slice(i * step, (i + 1) * step)
        own, other = turn(
            lambda n, f: expand((n, dense_near), (f, dense_far)),
            near_heads[0][rows],
            far_heads[0][rows],
            wait=(middle.other_far_y, third.far) if i == 0 else (),
        )
        state["dense"] = own, swap(other)
    third.both_to_x()
    middle.blocks(wait=(third.far_y, third.other_far, late.far))
    late.far_to_y()
    late.far_to_x()
    late.both_to_x()
    own_cotangent = away(to_local(masked))
    for i, state in enumerate(states):
        own, came = state["dense"]
        attn = own + came.astype(wide) + bias_dense
        first = ALPHA * own_tokens[i].astype(wide) + attn
        normal, scale = normalize(first)
        norm_one = normal * gain_one + shift_one
        norm_bf = norm_one.astype(narrow)
        state["one"] = normal, scale, norm_one
        state["norm_bf"] = norm_bf
        state["norm_rows"] = jnp.concatenate([norm_bf, swap(norm_bf)], axis=0)
    third.blocks(wait=[s["norm_bf"] for s in states] + [late.far_y, late.other_far])
    (full_gate,) = middle.weights()
    (full_upper,) = third.weights()
    for i, state in enumerate(states):
        state["ff"] = turn(
            ff_forward,
            state["norm_rows"],
            full_gate,
            full_upper,
            bias_gate,
            bias_upper,
            wait=(own_cotangent[1],) if i == 1 else (),
        )
    late.blocks()
    (full_down,) = late.weights()
    for state in states:
        own, other = turn(lambda r: expand((r, full_down)), state["ff"][2])
        state["down"] = own, swap(other)
    for i, state in enumerate(states):
        own, came = state["down"]
        mlp = own + came.astype(wide) + bias_down
        normal, scale = normalize(ALPHA * state["one"][2] + mlp)
        state["out"] = (normal * gain_two + shift_two).astype(narrow)
        grad_out = own_cotangent[i].astype(wide) * share
        grad_second = normalize_back(grad_out, gain_two, normal, scale)
        grad_mlp = grad_second.astype(narrow)
        state["second"] = grad_second
        state["came_mlp"] = swap(grad_mlp)
        state["mlp_rows"] = jnp.concatenate([grad_mlp, state["came_mlp"]], axis=0)
        state["vectors_two"] = (
            jnp.sum(grad_mlp.astype(wide), axis=0),
            jnp.sum(grad_out * normal, axis=0),
            jnp.sum(grad_out, axis=0),
        )

    layer_out, sent_out = home([s["out"] for s in states])

    def back_ff(state, wait=()):
        state["back"] = turn(
            ff_back, state["mlp_rows"], full_down, state["ff"][0], state["ff"][1], wait=wait
        )

    def back_up(state, wait=()):
        own, other = turn(
            lambda g, u: expand((g, full_gate), (u, full_upper)),
            state["back"][0],
            state["back"][1],
            wait=wait,
        )
        state["norm_grad"] = own, swap(other)

    def back_one(state):
        own, came = state["norm_grad"]
        normal, scale, _ = state["one"]
        grad_norm = ALPHA * state["second"] + own + came.astype(wide)
        grad_first = normalize_back(grad_norm, gain_one, normal, scale)
        grad_attn = grad_first.astype(narrow)
        state["first"] = grad_first
        state["grad_attn"] = grad_attn
        state["came_attn"] = swap(grad_attn)
        state["attn_rows"] = jnp.concatenate([grad_attn, state["came_attn"]], axis=0)
        state["vectors_one"] = (
            jnp.sum(grad_attn.astype(wide), axis=0),
            jnp.sum(grad_norm * normal, axis=0),
            jnp.sum(grad_norm, axis=0),
        )

    def chunks_of(pick):
        return [(pick(state), 0, step) for state in states]

    back_ff(states[0])
    back_up(states[0], wait=(states[1]["came_mlp"],))
    down = Reduction(chunks_of(lambda s: s["ff"][2]), chunks_of(lambda s: s["mlp_rows"]))
    down.to_core()
    back_ff(states[1])
    down.to_y(wait=(states[0]["norm_grad"][1],))
    back_one(states[0])
    back_up(states[1], wait=(states[0]["grad_attn"],))
    norm_all = chunks_of(lambda s: s["norm_rows"])
    gate = Reduction(chunks_of(lambda s: s["back"][0]), norm_all)
    upper = Reduction(chunks_of(lambda s: s["back"][1]), norm_all)
    gate.to_core(wait=(states[0]["came_attn"],))
    upper.to_core(wait=(down.came_y[1],))
    back_one(states[1])
    zero_row = jnp.zeros((1, heads * head_dim), wide)

    def back_dense(state, wait=()):
        return turn(project, state["attn_rows"], full_dense, zero_row, narrow, wait=wait)

    context_grads = [back_dense(states[0], wait=(states[1]["norm_grad"][1],))]
    upper.to_x_first(wait=(states[1]["grad_attn"],))
    gate.to_y(wait=(down.came_y[0],))
    context_grads.append(back_dense(states[1]))
    dense_grads = [
        HalfReduction(
            [(part[0], i, step) for i in range(CHUNKS)], chunks_of(lambda s: s["attn_rows"])
        )
        for part in (near_heads, far_heads)
    ]
    dense_grads[1].to_core(wait=(sent_out,))
    dense_grads[0].to_core()
    context_grad = jnp.concatenate(context_grads, axis=0)

    def back_heads(saved, first, wait=()):
        return turn(
            attend_back,
            context_grad,
            saved[1],
            saved[2],
            cos_table,
            sin_table,
            key_pos,
            query_pos,
            limit,
            first,
            shard_heads,
            head_dim,
            wait=wait,
        )

    def both_chunks(array):
        return [(array, i, step) for i in range(CHUNKS)]

    grad_far, bias_far = back_heads(far_heads, shard_heads)
    qkv_far = HalfReduction(both_chunks(grad_far), both_chunks(token_rows))
    qkv_far.to_core(wait=(upper.wide_far[1], gate.came_y[1]))
    down.to_x()
    grad_near, bias_near = back_heads(near_heads, 0, wait=(upper.wide_near[1],))
    upper.to_y_next()
    qkv_near = HalfReduction(both_chunks(grad_near), both_chunks(token_rows))

    grad_bias_qkv = jnp.concatenate([bias_near, bias_far], axis=0)
    grad_bias_gate = sum(s["back"][2] for s in states)
    grad_bias_upper = sum(s["back"][3] for s in states)

    def spread(values):
        cut = values.reshape(2, 2, -1)
        whole = jnp.zeros((n_tensor, values.size // 2), jnp.float32)
        whole = lax.dynamic_update_index_in_dim(whole, sides(cut[0, 0], cut[0, 1]), layer, 0)
        whole = lax.dynamic_update_index_in_dim(whole, sides(cut[1, 0], cut[1, 1]), layer ^ 2, 0)
        return whole.reshape(-1)

    stacked = jnp.stack(
        [sum(s[name][i] for s in states) for name in ("vectors_one", "vectors_two") for i in range(3)]
    ).reshape(6, 4, block_width)
    targets = place ^ jnp.arange(4, dtype=jnp.int32)
    targets = (((targets & 1) << 1) | (targets >> 1))[None, :, None]
    ordered = jnp.zeros_like(stacked)
    for position in range(4):
        ordered = jnp.where(targets == position, stacked[:, position : position + 1], ordered)
    def columns(values):
        rows = values.reshape(-1, 128)
        return jnp.pad(rows, ((0, -rows.shape[0] % 8), (0, 0)))

    small = [
        columns(ordered),
        columns(spread(grad_bias_qkv)),
        columns(spread(grad_bias_gate)),
        columns(spread(grad_bias_upper)),
    ]
    packed = pack(small)
    sums = [packed]
    for axis, hop in (("obj", 1), ("dp", 1), ("dp", 2), ("tensor", 1), ("tensor", 2)):
        moves = [(i, i ^ hop) for i in range(lax.axis_size(axis))]
        sums.append(sums[-1] + lax.ppermute(sums[-1], axis, moves))

    gate.to_x(wait=(gate.came_y[0],))
    down.to_far()
    qkv_near.to_core(wait=(down.far[1],))
    qkv_far.to_y(wait=(upper.far[1], sums[1]))
    half_count = full_qkv.count // 2
    weight_near = Weight(full_qkv.arrays, 0, half_count)
    weight_far = Weight(full_qkv.arrays, half_count, half_count)

    def back_qkv(i, wait=()):
        rows = slice(i * step, (i + 1) * step)
        own, other = turn(
            lambda n, f: expand((n, weight_near), (f, weight_far)),
            grad_near[rows],
            grad_far[rows],
            wait=wait,
        )
        states[i]["source"] = own, swap(other)

    back_qkv(0, wait=(upper.near[1], sums[2]))
    qkv_near.to_y(wait=(down.near[1], sums[3]))
    sum_down = down.finish()
    back_qkv(1, wait=(states[0]["source"][1], gate.far[1], sums[4]))
    gate.to_far()
    qkv_far.to_x(wait=(gate.near[1], sums[5]))
    dense_grads[1].to_y()
    dense_grads[0].to_y()
    came_qkv = back_far(add(*qkv_far.pair))
    qkv_near.to_x(wait=(states[1]["source"][1],))
    dense_grads[1].to_x()
    dense_grads[0].to_x()
    grad_inputs, _ = home(
        [
            (s["source"][0] + s["source"][1].astype(wide) + ALPHA * s["first"]).astype(narrow)
            for s in states
        ]
    )
    grad_inputs = grad_inputs.astype(wide)
    sum_gate = gate.finish()
    upper.to_far()
    mine_qkv = add(*qkv_near.pair, came_qkv)
    sum_qkv = sides(mine_qkv, back_x(mine_qkv)).astype(wide)
    came_dense = back_far(add(*dense_grads[1].pair))
    sum_upper = upper.finish()
    mine_dense = add(*dense_grads[0].pair, came_dense)
    sum_dense = sides(mine_dense, back_x(mine_dense)).astype(wide)
    norm_total = sums[-1][: small[0].shape[0]].reshape(6, width)
    flat_totals = []
    row = small[0].shape[0]
    for part, count in zip(small[1:], (n_qkv, shard_hidden, shard_hidden)):
        rows = sums[-1][row : row + count * n_tensor // 128]
        flat_totals.append(rows.reshape(-1))
        row += part.shape[0]
    total_qkv, total_gate, total_upper = flat_totals

    def own_shard(total, count):
        return lax.dynamic_slice_in_dim(total, layer * count, count)

    bias_total_qkv = own_shard(total_qkv, n_qkv).reshape(b_qkv.shape)
    bias_total_up = jnp.stack(
        [own_shard(total_gate, shard_hidden), own_shard(total_upper, shard_hidden)]
    )

    grad_w_qkv = sum_qkv.T.reshape(w_qkv.shape)
    grad_w_dense = sum_dense.reshape(w_dense.shape)
    grad_w_up = jnp.stack([sum_gate.T, sum_upper.T])
    grad_w_down = sum_down

    return (
        layer_out[None],
        grad_inputs[None],
        grad_w_qkv,
        bias_total_qkv,
        grad_w_dense,
        norm_total[0],
        norm_total[1],
        norm_total[2],
        grad_w_up,
        bias_total_up,
        grad_w_down,
        norm_total[3],
        norm_total[4],
        norm_total[5],
    )


def pair_plan_fits(mesh):
    return mesh.shape["obj"] == 2 and mesh.shape["dp"] == 4 and mesh.shape["tensor"] == 4


def solution(mesh):
    body = pair_shards if pair_plan_fits(mesh) else shards
    return jax.shard_map(
        body,
        mesh=mesh,
        in_specs=(
            P("obj", "dp", "tensor", None),
            P("obj", "dp", "tensor", None),
            P("obj", "dp", "tensor"),
            P("dp"),
            P(),
            P("dp", "tensor", None),
            P("tensor", None),
            P("tensor", None, "dp"),
            P(),
            P(),
            P(),
            P(None, "dp", "tensor"),
            P(None, "tensor"),
            P("tensor", "dp"),
            P(),
            P(),
            P(),
        ),
        out_specs=(
            P("obj", "dp", "tensor", None),
            P("obj", "dp", "tensor", None),
            P("dp", "tensor", None),
            P("tensor", None),
            P("tensor", None, "dp"),
            P(),
            P(),
            P(),
            P(None, "dp", "tensor"),
            P(None, "tensor"),
            P("tensor", "dp"),
            P(),
            P(),
            P(),
        ),
        check_vma=False,
    )
```

```python
import math

import jax
import jax.numpy as jnp
from jax import lax
from jax.experimental import pallas as pl
from jax.experimental.pallas import tpu as pltpu
from jax.sharding import PartitionSpec as P

ALPHA = 48.0**0.5
epsilon = 1e-05


def rotary(source):
    length = source.shape[0]
    half_dim = source.shape[-1] // 2
    frequency = 10000.0 ** (-2.0 * jnp.arange(half_dim, dtype=jnp.float32) / source.shape[-1])
    angles = jnp.arange(length, dtype=jnp.float32)[:, None] * frequency[None, :]
    cosine = jnp.cos(angles)[:, None, :]
    sine_table = jnp.sin(angles)[:, None, :]
    first_half = source[..., :half_dim]
    second = source[..., half_dim:]
    return jnp.concatenate(
        [first_half * cosine - second * sine_table, second * cosine + first_half * sine_table],
        axis=-1,
    )


def rope_pair(query_pre, key_pre):
    return (rotary(query_pre), rotary(key_pre))


def layer_norm(source, gain_vec, shift_vec):
    centred = source - jnp.mean(source, axis=-1, keepdims=True)
    variance = jnp.mean(centred * centred, axis=-1, keepdims=True)
    return centred * lax.rsqrt(variance + epsilon) * gain_vec + shift_vec


def geglu(gate_part, up_part):
    return jax.nn.gelu(gate_part) * up_part


def block_scores(query_block, key_bf, start, prefix_length, score_scale):
    length = key_bf.shape[0]
    scores = (
        jnp.einsum("qhd,khd->hqk", query_block, key_bf, preferred_element_type=jnp.float32)
        * score_scale
    )
    query_pos = start + jnp.arange(query_block.shape[0], dtype=jnp.int32)
    key_pos = jnp.arange(length, dtype=jnp.int32)
    visible = (key_pos[None, :] < prefix_length) | (key_pos[None, :] <= query_pos[:, None])
    return jnp.where(visible[None], scores, -1e30)


def shards(
    tokens,
    cotangent,
    loss_mask,
    prefix,
    counts,
    w_qkv,
    b_qkv,
    w_dense,
    b_dense,
    ln1_gain,
    ln1_bias,
    w_up,
    b_up,
    w_down,
    b_down,
    ln2_gain,
    ln2_bias,
):
    item_count = tokens.shape[1]
    row_count = tokens.shape[2]
    model_width = tokens.shape[3]
    length = row_count * lax.axis_size("tensor")
    local_heads = w_qkv.shape[1]
    head_dim = w_qkv.shape[2] // 3
    local_hidden = w_up.shape[2]
    block_rows = min(512, length)
    score_scale = head_dim ** (-0.5)
    group_id = lax.axis_index("obj")
    count_float = counts.astype(jnp.float32)
    share = jnp.where(group_id == 0, count_float[0], count_float[1]) / (
        count_float[0] + count_float[1]
    )
    bias_qkv = b_qkv.astype(jnp.float32)
    bias_dense = b_dense.astype(jnp.float32)
    gain_one = ln1_gain.astype(jnp.float32)
    shift_one = ln1_bias.astype(jnp.float32)
    bias_up = b_up.astype(jnp.float32)
    bias_down = b_down.astype(jnp.float32)
    gain_two = ln2_gain.astype(jnp.float32)
    shift_two = ln2_bias.astype(jnp.float32)

    def fetch():
        return (
            lax.all_gather(w_qkv, "dp", axis=0, tiled=True),
            lax.all_gather(w_dense, "dp", axis=2, tiled=True),
            lax.all_gather(w_up, "dp", axis=1, tiled=True),
            lax.all_gather(w_down, "dp", axis=1, tiled=True),
        )

    def one_item(item_slot, carry):
        outputs, grad_inputs, large_grads, bias_grads, norm_grads = carry
        qkv_full, dense_full, up_full, down_full = fetch()
        token_rows = lax.dynamic_index_in_dim(tokens[0], item_slot, 0, keepdims=False)
        prefix_length = jnp.where(group_id == 0, length, prefix[item_slot])
        gathered = lax.all_gather(token_rows, "tensor", axis=0, tiled=True)
        projected = (
            jnp.einsum("ld,dhe->lhe", gathered, qkv_full, preferred_element_type=jnp.float32)
            + bias_qkv
        )
        (query_rot, key_rot), rope_pull = jax.vjp(
            rope_pair, projected[..., :head_dim], projected[..., head_dim : 2 * head_dim]
        )
        query_bf = query_rot.astype(jnp.bfloat16)
        key_bf = key_rot.astype(jnp.bfloat16)
        value_bf = projected[..., 2 * head_dim :].astype(jnp.bfloat16)
        context_parts = []
        lse_parts = []
        for start in range(0, length, block_rows):
            scores = block_scores(
                query_bf[start : start + block_rows], key_bf, start, prefix_length, score_scale
            )
            highest_score = jnp.max(scores, axis=-1, keepdims=True)
            expo = jnp.exp(scores - highest_score)
            totals = jnp.sum(expo, axis=-1, keepdims=True)
            soft_weights = (expo / totals).astype(jnp.bfloat16)
            context_parts.append(
                jnp.einsum(
                    "hqk,khd->qhd", soft_weights, value_bf, preferred_element_type=jnp.float32
                )
            )
            lse_parts.append((highest_score + jnp.log(totals))[..., 0])
        context_bf = jnp.concatenate(context_parts, axis=0).astype(jnp.bfloat16)
        log_totals = jnp.concatenate(lse_parts, axis=1)
        source = token_rows.astype(jnp.float32)
        piece = lax.slice_in_dim(context_bf, 0, lax.axis_size("tensor") * row_count, axis=0)
        attn_rows = (
            lax.psum_scatter(
                jnp.einsum("lhd,hde->le", piece, dense_full, preferred_element_type=jnp.float32),
                "tensor",
                scatter_dimension=0,
                tiled=True,
            )
            + bias_dense
        )
        first_norm, norm_one_pull = jax.vjp(
            layer_norm, ALPHA * source + attn_rows, gain_one, shift_one
        )
        norm_full = lax.all_gather(first_norm.astype(jnp.bfloat16), "tensor", axis=0, tiled=True)
        gate_up = (
            jnp.einsum("ld,kdf->klf", norm_full, up_full, preferred_element_type=jnp.float32)
            + bias_up[:, None, :]
        )
        activated, act_pull = jax.vjp(geglu, gate_up[0], gate_up[1])
        hidden_bf = activated.astype(jnp.bfloat16)
        piece = lax.slice_in_dim(hidden_bf, 0, lax.axis_size("tensor") * row_count, axis=0)
        mlp_rows = (
            lax.psum_scatter(
                jnp.dot(piece, down_full, preferred_element_type=jnp.float32),
                "tensor",
                scatter_dimension=0,
                tiled=True,
            )
            + bias_down
        )
        result, norm_two_pull = jax.vjp(
            layer_norm, ALPHA * first_norm + mlp_rows, gain_two, shift_two
        )
        qkv_back, dense_back, up_back, down_back = fetch()
        mask_rows = lax.dynamic_index_in_dim(loss_mask[0], item_slot, 0, keepdims=False).astype(
            jnp.float32
        )
        cot_rows = lax.dynamic_index_in_dim(cotangent[0], item_slot, 0, keepdims=False).astype(
            jnp.float32
        )
        grad_out = cot_rows * mask_rows[:, None] * share
        grad_second, grad_gain_two, grad_shift_two = norm_two_pull(grad_out)
        grad_mlp = grad_second.astype(jnp.bfloat16)
        grad_bias_down = jnp.sum(grad_mlp.astype(jnp.float32), axis=0)
        grad_mlp_full = lax.all_gather(grad_mlp, "tensor", axis=0, tiled=True)
        grad_down = jnp.einsum(
            "lf,ld->fd", hidden_bf, grad_mlp_full, preferred_element_type=jnp.float32
        )
        grad_hidden = jnp.einsum(
            "ld,fd->lf", grad_mlp_full, down_back, preferred_element_type=jnp.float32
        )
        grad_gate, grad_upper = act_pull(grad_hidden)
        grad_gate_up = jnp.stack([grad_gate, grad_upper]).astype(jnp.bfloat16)
        grad_bias_up = jnp.sum(grad_gate_up.astype(jnp.float32), axis=1)
        grad_up = jnp.einsum(
            "ld,klf->kdf", norm_full, grad_gate_up, preferred_element_type=jnp.float32
        )
        piece = lax.slice_in_dim(grad_gate_up, 0, lax.axis_size("tensor") * row_count, axis=1)
        grad_norm_one = ALPHA * grad_second + lax.psum_scatter(
            jnp.einsum("klf,kdf->ld", piece, up_back, preferred_element_type=jnp.float32),
            "tensor",
            scatter_dimension=0,
            tiled=True,
        )
        grad_first, grad_gain_one, grad_shift_one = norm_one_pull(grad_norm_one)
        grad_attn = grad_first.astype(jnp.bfloat16)
        grad_bias_dense = jnp.sum(grad_attn.astype(jnp.float32), axis=0)
        grad_attn_full = lax.all_gather(grad_attn, "tensor", axis=0, tiled=True)
        grad_dense = jnp.einsum(
            "lhd,le->hde", context_bf, grad_attn_full, preferred_element_type=jnp.float32
        )
        grad_context = jnp.einsum(
            "le,hde->lhd", grad_attn_full, dense_back, preferred_element_type=jnp.float32
        ).astype(jnp.bfloat16)
        query_grads = []
        key_grad = jnp.zeros((length, local_heads, head_dim), jnp.float32)
        value_grad = jnp.zeros((length, local_heads, head_dim), jnp.float32)
        for start in range(0, length, block_rows):
            query_block = query_bf[start : start + block_rows]
            scores = block_scores(query_block, key_bf, start, prefix_length, score_scale)
            soft_full = jnp.exp(scores - log_totals[:, start : start + block_rows, None])
            context_block = grad_context[start : start + block_rows]
            grad_soft = jnp.einsum(
                "qhd,khd->hqk", context_block, value_bf, preferred_element_type=jnp.float32
            )
            grad_scores = (
                soft_full * (grad_soft - jnp.sum(soft_full * grad_soft, axis=-1, keepdims=True))
            ).astype(jnp.bfloat16)
            query_grads.append(
                jnp.einsum("hqk,khd->qhd", grad_scores, key_bf, preferred_element_type=jnp.float32)
                * score_scale
            )
            key_grad = (
                key_grad
                + jnp.einsum(
                    "hqk,qhd->khd", grad_scores, query_block, preferred_element_type=jnp.float32
                )
                * score_scale
            )
            value_grad = value_grad + jnp.einsum(
                "hqk,qhd->khd",
                soft_full.astype(jnp.bfloat16),
                context_block,
                preferred_element_type=jnp.float32,
            )
        grad_query_pre, grad_key_pre = rope_pull((jnp.concatenate(query_grads, axis=0), key_grad))
        grad_projected = jnp.concatenate(
            [grad_query_pre, grad_key_pre, value_grad], axis=-1
        ).astype(jnp.bfloat16)
        grad_bias_qkv = jnp.sum(grad_projected.astype(jnp.float32), axis=0)
        grad_qkv = jnp.einsum(
            "ld,lhe->dhe", gathered, grad_projected, preferred_element_type=jnp.float32
        )
        piece = lax.slice_in_dim(grad_projected, 0, row_count * lax.axis_size("tensor"), axis=0)
        grad_source = ALPHA * grad_first + lax.psum_scatter(
            jnp.einsum("lhe,dhe->ld", piece, qkv_back, preferred_element_type=jnp.float32).astype(
                jnp.bfloat16
            ),
            "tensor",
            scatter_dimension=0,
            tiled=True,
        ).astype(jnp.float32)
        outputs = lax.dynamic_update_index_in_dim(
            outputs, result.astype(jnp.bfloat16), item_slot, 0
        )
        grad_inputs = lax.dynamic_update_index_in_dim(grad_inputs, grad_source, item_slot, 0)
        large_grads = (
            large_grads[0] + grad_qkv,
            large_grads[1] + grad_dense,
            large_grads[2] + grad_up,
            large_grads[3] + grad_down,
        )
        bias_grads = (bias_grads[0] + grad_bias_qkv, bias_grads[1] + grad_bias_up)
        norm_grads = (
            norm_grads[0] + grad_bias_dense,
            norm_grads[1] + grad_gain_one,
            norm_grads[2] + grad_shift_one,
            norm_grads[3] + grad_bias_down,
            norm_grads[4] + grad_gain_two,
            norm_grads[5] + grad_shift_two,
        )
        return (outputs, grad_inputs, large_grads, bias_grads, norm_grads)

    zero_vector = jnp.zeros((model_width,), jnp.float32)
    initial = (
        jnp.zeros((item_count, row_count, model_width), jnp.bfloat16),
        jnp.zeros((item_count, row_count, model_width), jnp.float32),
        (
            jnp.zeros((model_width, local_heads, 3 * head_dim), jnp.float32),
            jnp.zeros((local_heads, head_dim, model_width), jnp.float32),
            jnp.zeros((2, model_width, local_hidden), jnp.float32),
            jnp.zeros((local_hidden, model_width), jnp.float32),
        ),
        (
            jnp.zeros((local_heads, 3 * head_dim), jnp.float32),
            jnp.zeros((2, local_hidden), jnp.float32),
        ),
        (zero_vector, zero_vector, zero_vector, zero_vector, zero_vector, zero_vector),
    )
    outputs, grad_inputs, large_grads, bias_grads, norm_grads = lax.fori_loop(
        0, item_count, one_item, initial
    )
    sharded = (
        lax.psum_scatter(
            large_grads[0].astype(jnp.bfloat16), "dp", scatter_dimension=0, tiled=True
        ).astype(jnp.float32),
        lax.psum_scatter(
            large_grads[1].astype(jnp.bfloat16), "dp", scatter_dimension=2, tiled=True
        ).astype(jnp.float32),
        lax.psum_scatter(
            large_grads[2].astype(jnp.bfloat16), "dp", scatter_dimension=1, tiled=True
        ).astype(jnp.float32),
        lax.psum_scatter(
            large_grads[3].astype(jnp.bfloat16), "dp", scatter_dimension=1, tiled=True
        ).astype(jnp.float32),
    )
    merged = (
        lax.psum(sharded[0].astype(jnp.bfloat16), "obj").astype(jnp.float32),
        lax.psum(sharded[1].astype(jnp.bfloat16), "obj").astype(jnp.float32),
        lax.psum(sharded[2].astype(jnp.bfloat16), "obj").astype(jnp.float32),
        lax.psum(sharded[3].astype(jnp.bfloat16), "obj").astype(jnp.float32),
    )
    bias_total = lax.psum((bias_grads[0], bias_grads[1]), ("obj", "dp"))
    norm_total = lax.psum(
        (norm_grads[0], norm_grads[1], norm_grads[2], norm_grads[3], norm_grads[4], norm_grads[5]),
        ("obj", "dp", "tensor"),
    )
    return (
        outputs[None],
        grad_inputs[None],
        merged[0],
        bias_total[0],
        merged[1],
        norm_total[0],
        norm_total[1],
        norm_total[2],
        merged[2],
        bias_total[1],
        merged[3],
        norm_total[3],
        norm_total[4],
        norm_total[5],
    )


def paced(flops):
    return pl.CostEstimate(flops=int(flops / 2), bytes_accessed=1, transcendentals=0)


def attend(projected, cos_table, sin_table, key_pos, query_pos, limit, first, heads, head_dim):
    length = projected.shape[0]
    block = min(256, length)
    score_scale = head_dim ** (-0.5)
    half_dim = head_dim // 2

    def kernel(limit_ref, proj_ref, cos_ref, sin_ref, kpos_ref, qpos_ref, ctx_ref, qkv_ref, lse_ref):
        cosine = cos_ref[...]
        sine = sin_ref[...]
        query = proj_ref[:, :head_dim].astype(jnp.float32)
        key = proj_ref[:, head_dim : 2 * head_dim].astype(jnp.float32)
        query = query * cosine + pltpu.roll(query, half_dim, 1) * sine
        key = key * cosine + pltpu.roll(key, half_dim, 1) * sine
        qkv_ref[:, :head_dim] = query.astype(jnp.bfloat16)
        key_bf = key.astype(jnp.bfloat16)
        qkv_ref[:, head_dim : 2 * head_dim] = key_bf
        value_bf = proj_ref[:, 2 * head_dim :].astype(jnp.bfloat16)
        qkv_ref[:, 2 * head_dim :] = value_bf
        prefix_length = limit_ref[0]
        near = kpos_ref[...] < prefix_length
        for start in range(0, length, block):
            rows = slice(start, start + block)
            scores = (
                lax.dot_general(
                    key_bf,
                    qkv_ref[rows, :head_dim],
                    (((1,), (1,)), ((), ())),
                    preferred_element_type=jnp.float32,
                )
                * score_scale
            )
            visible = near | (kpos_ref[...] <= qpos_ref[:, rows])
            scores = jnp.where(visible, scores, -1e30)
            highest_score = jnp.max(scores, axis=0, keepdims=True)
            expo = jnp.exp(scores - highest_score)
            totals = jnp.sum(expo, axis=0, keepdims=True)
            weights = (expo / totals).astype(jnp.bfloat16)
            ctx_ref[rows, :] = lax.dot_general(
                weights,
                value_bf,
                (((0,), (0,)), ((), ())),
                preferred_element_type=jnp.float32,
            ).astype(jnp.bfloat16)
            lse_ref[0, :, rows] = highest_score + jnp.log(totals)

    fixed = lambda h, lim: (0, 0)
    return pl.pallas_call(
        kernel,
        grid_spec=pltpu.PrefetchScalarGridSpec(
            num_scalar_prefetch=1,
            grid=(heads,),
            in_specs=[
                pl.BlockSpec((length, 3 * head_dim), lambda h, lim: (0, h + first)),
                pl.BlockSpec((length, head_dim), fixed),
                pl.BlockSpec((length, head_dim), fixed),
                pl.BlockSpec((length, 1), fixed),
                pl.BlockSpec((1, length), fixed),
            ],
            out_specs=[
                pl.BlockSpec((length, head_dim), lambda h, lim: (0, h)),
                pl.BlockSpec((length, 3 * head_dim), lambda h, lim: (0, h)),
                pl.BlockSpec((1, 1, length), lambda h, lim: (h, 0, 0)),
            ],
        ),
        out_shape=[
            jax.ShapeDtypeStruct((length, heads * head_dim), jnp.bfloat16),
            jax.ShapeDtypeStruct((length, heads * 3 * head_dim), jnp.bfloat16),
            jax.ShapeDtypeStruct((heads, 1, length), jnp.float32),
        ],
        compiler_params=pltpu.CompilerParams(vmem_limit_bytes=48 * 1024 * 1024),
        cost_estimate=paced(8 * heads * length * length * head_dim),
        name="attend",
    )(limit, projected, cos_table, sin_table, key_pos, query_pos)


def attend_back(
    grad_contexts,
    qkv,
    log_totals,
    cos_table,
    sin_table,
    key_pos,
    query_pos,
    limit,
    first,
    heads,
    head_dim,
):
    length = qkv.shape[0]
    block = min(256, length // 2)
    score_scale = head_dim ** (-0.5)
    half_dim = head_dim // 2

    def kernel(
        limit_ref,
        qkv_ref,
        grad_first,
        grad_second,
        lse_ref,
        cos_ref,
        sin_ref,
        kpos_ref,
        qpos_ref,
        out_ref,
        bias_ref,
        query_grad,
        key_grad,
        value_grad,
    ):
        key_bf = qkv_ref[:, head_dim : 2 * head_dim]
        value_bf = qkv_ref[:, 2 * head_dim :]
        prefix_length = limit_ref[0]
        near = kpos_ref[...] < prefix_length
        for start in range(0, length, block):
            rows = slice(start, start + block)
            query_block = qkv_ref[rows, :head_dim]
            grad_ref = grad_first if start < length // 2 else grad_second
            shift = start % (length // 2)
            grad_block = grad_ref[shift : shift + block, :]
            scores = (
                lax.dot_general(
                    key_bf,
                    query_block,
                    (((1,), (1,)), ((), ())),
                    preferred_element_type=jnp.float32,
                )
                * score_scale
            )
            visible = near | (kpos_ref[...] <= qpos_ref[:, rows])
            soft = jnp.exp(jnp.where(visible, scores, -1e30) - lse_ref[0, :, rows])
            grad_soft = lax.dot_general(
                value_bf,
                grad_block,
                (((1,), (1,)), ((), ())),
                preferred_element_type=jnp.float32,
            )
            inner = jnp.sum(soft * grad_soft, axis=0, keepdims=True)
            grad_scores = (soft * (grad_soft - inner)).astype(jnp.bfloat16)
            query_grad[rows, :] = (
                lax.dot_general(
                    grad_scores,
                    key_bf,
                    (((0,), (0,)), ((), ())),
                    preferred_element_type=jnp.float32,
                )
                * score_scale
            )
            key_term = (
                jnp.dot(grad_scores, query_block, preferred_element_type=jnp.float32) * score_scale
            )
            value_term = jnp.dot(
                soft.astype(jnp.bfloat16), grad_block, preferred_element_type=jnp.float32
            )
            if start == 0:
                key_grad[...] = key_term
                value_grad[...] = value_term
            else:
                key_grad[...] += key_term
                value_grad[...] += value_term
        cosine = cos_ref[...]
        sine = sin_ref[...]
        turned = query_grad[...]
        turned = (turned * cosine + pltpu.roll(turned * sine, half_dim, 1)).astype(jnp.bfloat16)
        out_ref[:, :head_dim] = turned
        bias_ref[0, :, :head_dim] = jnp.sum(turned.astype(jnp.float32), axis=0, keepdims=True)
        turned = key_grad[...]
        turned = (turned * cosine + pltpu.roll(turned * sine, half_dim, 1)).astype(jnp.bfloat16)
        out_ref[:, head_dim : 2 * head_dim] = turned
        bias_ref[0, :, head_dim : 2 * head_dim] = jnp.sum(
            turned.astype(jnp.float32), axis=0, keepdims=True
        )
        turned = value_grad[...].astype(jnp.bfloat16)
        out_ref[:, 2 * head_dim :] = turned
        bias_ref[0, :, 2 * head_dim :] = jnp.sum(turned.astype(jnp.float32), axis=0, keepdims=True)

    fixed = lambda h, lim: (0, 0)
    return pl.pallas_call(
        kernel,
        grid_spec=pltpu.PrefetchScalarGridSpec(
            num_scalar_prefetch=1,
            grid=(heads,),
            in_specs=[
                pl.BlockSpec((length, 3 * head_dim), lambda h, lim: (0, h)),
                pl.BlockSpec((length // 2, head_dim), lambda h, lim: (0, h + first)),
                pl.BlockSpec((length // 2, head_dim), lambda h, lim: (0, h + first)),
                pl.BlockSpec((1, 1, length), lambda h, lim: (h, 0, 0)),
                pl.BlockSpec((length, head_dim), fixed),
                pl.BlockSpec((length, head_dim), fixed),
                pl.BlockSpec((length, 1), fixed),
                pl.BlockSpec((1, length), fixed),
            ],
            out_specs=[
                pl.BlockSpec((length, 3 * head_dim), lambda h, lim: (0, h)),
                pl.BlockSpec((1, 1, 3 * head_dim), lambda h, lim: (h, 0, 0)),
            ],
            scratch_shapes=[pltpu.VMEM((length, head_dim), jnp.float32)] * 3,
        ),
        out_shape=[
            jax.ShapeDtypeStruct((length, heads * 3 * head_dim), jnp.bfloat16),
            jax.ShapeDtypeStruct((heads, 1, 3 * head_dim), jnp.float32),
        ],
        compiler_params=pltpu.CompilerParams(vmem_limit_bytes=48 * 1024 * 1024),
        cost_estimate=paced(10 * heads * length * length * head_dim),
        name="attend_back",
    )(limit, qkv, *grad_contexts, log_totals, cos_table, sin_table, key_pos, query_pos)


def transposed_dot(left, right):
    return lax.dot_general(
        left, right, (((1,), (1,)), ((), ())), preferred_element_type=jnp.float32
    )


def rows_outer(features, right):
    return lax.dot_general(
        features, right, (((0,), (0,)), ((), ())), preferred_element_type=jnp.float32
    )


VMEM_BYTES = 60 * 1024 * 1024


def join(parts, count, target, total, offset):
    width = parts[0][0].shape[1]
    rows = count
    while offset % rows or any(first % rows for _, first in parts):
        rows //= 2
    steps = count // rows

    def kernel(*refs):
        for index in range(4):

            @pl.when(pl.program_id(1) == index)
            def _():
                refs[-1][...] = refs[index][...]

    def source(first):
        return pl.BlockSpec((rows, width), lambda i, p: (first // rows + i, 0))

    given = [] if target is None else [target]
    return pl.pallas_call(
        kernel,
        grid=(steps, 4),
        in_specs=[source(first) for _, first in parts]
        + [pl.BlockSpec(memory_space=pl.ANY)] * len(given),
        out_specs=pl.BlockSpec((rows, width), lambda i, p: (offset // rows + p * steps + i, 0)),
        out_shape=jax.ShapeDtypeStruct((total, width), parts[0][0].dtype),
        input_output_aliases={4: 0} if given else {},
        compiler_params=pltpu.CompilerParams(vmem_limit_bytes=VMEM_BYTES),
        cost_estimate=paced(1000 * count * width),
        name="join",
    )(*[array for array, _ in parts], *given)


def block_of(count, sizes=(512, 256, 128)):
    for size in sizes:
        if count % size == 0:
            return size
    return count


class Weight:
    def __init__(self, arrays, count):
        self.arrays = [array for array, _ in arrays]
        self.starts = [start for _, start in arrays]
        self.count = count
        self.part = self.arrays[0].shape[1]
        self.width = 4 * self.part

    def rows(self, first, count):
        moved = [start + first for start in self.starts]
        return Weight(list(zip(self.arrays, moved)), count)

    def row_specs(self, block):
        def spec(start):
            return pl.BlockSpec((block, self.part), lambda j: (start // block + j, 0))

        return [spec(start) for start in self.starts]


def project_block(rows_ref, weight_refs):
    total = None
    for index, ref in enumerate(weight_refs):
        part = ref.shape[1]
        product = transposed_dot(rows_ref[:, index * part : (index + 1) * part], ref[...])
        total = product if total is None else total + product
    return total


def gather_rows(piece_refs, rows_ref):
    @pl.when(pl.program_id(0) == 0)
    def _():
        row = 0
        for ref in piece_refs:
            rows_ref[row : row + ref.shape[0]] = ref[...]
            row += ref.shape[0]


def piece_specs(pieces):
    return [pl.BlockSpec(piece.shape, lambda j: (0, 0)) for piece in pieces]


def project(pieces, weight, bias, kind):
    width = pieces[0].shape[1]
    count = sum(piece.shape[0] for piece in pieces)
    features = weight.count
    block = block_of(features)
    given = len(pieces)

    def kernel(*refs):
        gather_rows(refs[:given], refs[-1])
        w0, w1, w2, w3, bias_ref, out_ref, rows_ref = refs[given:]
        result = project_block(rows_ref, (w0, w1, w2, w3))
        out_ref[...] = (result + bias_ref[...]).astype(kind)

    return pl.pallas_call(
        kernel,
        grid=(features // block,),
        in_specs=piece_specs(pieces)
        + weight.row_specs(block)
        + [pl.BlockSpec((1, block), lambda j: (0, j))],
        out_specs=pl.BlockSpec((count, block), lambda j: (0, j)),
        out_shape=jax.ShapeDtypeStruct((count, features), kind),
        scratch_shapes=[pltpu.VMEM((count, width), jnp.bfloat16)],
        compiler_params=pltpu.CompilerParams(vmem_limit_bytes=VMEM_BYTES),
        cost_estimate=paced(2 * count * width * features),
        name="project",
    )(*pieces, *weight.arrays, bias)


def ff_forward(pieces, gate_weight, upper_weight, bias_gate, bias_upper):
    width = pieces[0].shape[1]
    count = sum(piece.shape[0] for piece in pieces)
    features = gate_weight.count
    block = block_of(features)
    given = len(pieces)

    def kernel(*refs):
        gather_rows(refs[:given], refs[-1])
        refs = refs[given:]
        bg_ref, bu_ref, gate_ref, upper_ref, hid_ref, rows_ref = refs[8:]
        gate = project_block(rows_ref, refs[:4]) + bg_ref[...]
        upper = project_block(rows_ref, refs[4:8]) + bu_ref[...]
        gate_ref[...] = gate.astype(jnp.bfloat16)
        upper_ref[...] = upper.astype(jnp.bfloat16)
        hid_ref[...] = (jax.nn.gelu(gate) * upper).astype(jnp.bfloat16)

    out = jax.ShapeDtypeStruct((count, features), jnp.bfloat16)
    return pl.pallas_call(
        kernel,
        grid=(features // block,),
        in_specs=piece_specs(pieces)
        + gate_weight.row_specs(block)
        + upper_weight.row_specs(block)
        + [pl.BlockSpec((1, block), lambda j: (0, j))] * 2,
        out_specs=[pl.BlockSpec((count, block), lambda j: (0, j))] * 3,
        out_shape=[out, out, out],
        scratch_shapes=[pltpu.VMEM((count, width), jnp.bfloat16)],
        compiler_params=pltpu.CompilerParams(vmem_limit_bytes=VMEM_BYTES),
        cost_estimate=paced(4 * count * width * features),
        name="ff_forward",
    )(*pieces, *gate_weight.arrays, *upper_weight.arrays, bias_gate, bias_upper)


def ff_back(pieces, down_weight, gate, upper):
    width = pieces[0].shape[1]
    count = sum(piece.shape[0] for piece in pieces)
    features = down_weight.count
    block = block_of(features)
    factor = (2.0 / math.pi) ** 0.5
    given = len(pieces)

    def kernel(*refs):
        gather_rows(refs[:given], refs[-1])
        w0, w1, w2, w3, gate_ref, upper_ref, gg_ref, gu_ref, sg_ref, su_ref, rows_ref = refs[given:]
        grad = project_block(rows_ref, (w0, w1, w2, w3))
        value = gate_ref[...].astype(jnp.float32)
        square = value * value
        bend = jnp.tanh(factor * value * (1.0 + 0.044715 * square))
        lift = 0.5 * (1.0 + bend)
        slope = lift + 0.5 * value * (1.0 - bend * bend) * (
            factor * (1.0 + 3.0 * 0.044715 * square)
        )
        grad_gate = (grad * upper_ref[...].astype(jnp.float32) * slope).astype(jnp.bfloat16)
        grad_upper = (grad * (value * lift)).astype(jnp.bfloat16)
        gg_ref[...] = grad_gate
        gu_ref[...] = grad_upper
        sg_ref[...] = jnp.sum(grad_gate.astype(jnp.float32), axis=0, keepdims=True)
        su_ref[...] = jnp.sum(grad_upper.astype(jnp.float32), axis=0, keepdims=True)

    out = jax.ShapeDtypeStruct((count, features), jnp.bfloat16)
    row = jax.ShapeDtypeStruct((1, features), jnp.float32)
    return pl.pallas_call(
        kernel,
        grid=(features // block,),
        in_specs=piece_specs(pieces)
        + down_weight.row_specs(block)
        + [pl.BlockSpec((count, block), lambda j: (0, j))] * 2,
        out_specs=[pl.BlockSpec((count, block), lambda j: (0, j))] * 2
        + [pl.BlockSpec((1, block), lambda j: (0, j))] * 2,
        out_shape=[out, out, row, row],
        scratch_shapes=[pltpu.VMEM((count, width), jnp.bfloat16)],
        compiler_params=pltpu.CompilerParams(vmem_limit_bytes=VMEM_BYTES),
        cost_estimate=paced(3 * count * width * features),
        name="ff_back",
    )(*pieces, *down_weight.arrays, gate, upper)


def expand(*pairs):
    count = pairs[0][0][2]
    width = pairs[0][1].width
    part = width // 4
    own = count // 2
    terms = len(pairs)
    cuts = 2 if sum(weight.count for _, weight in pairs) > 4000 else 1
    block = part // cuts

    def kernel(*refs):
        own_ref, other_ref = refs[5 * terms :]
        for which in range(4):

            @pl.when(pl.program_id(0) // cuts == which)
            def _():
                total = None
                for term in range(terms):
                    product = jnp.dot(
                        refs[5 * term][...],
                        refs[5 * term + 1 + which][...],
                        preferred_element_type=jnp.float32,
                    )
                    total = product if total is None else total + product
                own_ref[...] = total[:own]
                other_ref[...] = total[own:].astype(jnp.bfloat16)

    def column(weight, which):
        return pl.BlockSpec(
            (weight.count, block),
            lambda j: (
                weight.starts[which] // weight.count,
                jnp.clip(j - cuts * which, 0, cuts - 1),
            ),
        )

    specs = []
    operands = []
    def row_block(depth, row):
        return pl.BlockSpec((count, depth), lambda j: (row, 0))

    for (features, row, _), weight in pairs:
        specs.append(row_block(weight.count, row))
        specs += [column(weight, which) for which in range(4)]
        operands += [features, *weight.arrays]
    return pl.pallas_call(
        kernel,
        grid=(4 * cuts,),
        in_specs=specs,
        out_specs=[pl.BlockSpec((own, block), lambda j: (0, j))] * 2,
        out_shape=[
            jax.ShapeDtypeStruct((own, width), jnp.float32),
            jax.ShapeDtypeStruct((own, width), jnp.bfloat16),
        ],
        compiler_params=pltpu.CompilerParams(vmem_limit_bytes=VMEM_BYTES),
        cost_estimate=paced(2 * count * width * sum(weight.count for _, weight in pairs)),
        name="expand",
    )(*operands)


def outer(features, rights, start, columns, parts, added=(), pieces=(), steps=2):
    chunks = len(features)
    count = features[0][2]
    given = len(rights)
    total = features[0][0].shape[1]
    block = total // steps
    rows = total // parts

    def kernel(*refs):
        gather_rows(refs[chunks : chunks + given], refs[-1])
        result = None
        for chunk in range(chunks):
            rows_here = refs[-1][chunk * count : (chunk + 1) * count]
            product = rows_outer(refs[chunk][...], rows_here)
            result = product if result is None else result + product
        first = chunks + given
        for ref in refs[first : first + len(added)]:
            result = result + ref[...].astype(jnp.float32)
        first += len(added)
        outs = refs[first + len(pieces) : -1]
        if parts == 1:
            outs[0][...] = result.astype(jnp.bfloat16)
            return
        each = parts // steps
        for half in range(steps):

            @pl.when(pl.program_id(0) == half)
            def _():
                whole = result
                if pieces:
                    whole = whole + refs[first + half][...].astype(jnp.float32)
                whole = whole.astype(jnp.bfloat16)
                for index in range(each):
                    outs[half * each + index][...] = whole[index * rows : (index + 1) * rows]

    def at(row, column):
        return lambda j: (row, column)

    def across(row):
        return lambda j: (row, j)

    def along(column):
        return lambda j: (j, column)

    if parts == 1:
        out_specs = [pl.BlockSpec((block, columns), along(0))]
    else:
        out_specs = [pl.BlockSpec((rows, columns), at(0, 0))] * parts
    return pl.pallas_call(
        kernel,
        grid=(steps,),
        in_specs=[pl.BlockSpec((count, block), across(row)) for _, row, _ in features]
        + [pl.BlockSpec((right.shape[0], columns), at(0, start // columns)) for right in rights]
        + [pl.BlockSpec((block, columns), along(column // columns)) for _, column in added]
        + [pl.BlockSpec((block, columns), at(0, 0))] * len(pieces),
        out_specs=out_specs,
        out_shape=[jax.ShapeDtypeStruct((rows, columns), jnp.bfloat16)] * parts,
        scratch_shapes=[pltpu.VMEM((chunks * count, columns), jnp.bfloat16)],
        compiler_params=pltpu.CompilerParams(vmem_limit_bytes=VMEM_BYTES),
        cost_estimate=paced(6 * chunks * count * total * columns),
        name="outer",
    )(
        *[array for array, _, _ in features],
        *rights,
        *[array for array, _ in added],
        *pieces,
    )


def after(values, *earlier):
    return lax.optimization_barrier((values,) + earlier)[0]


CHUNKS = 2


def pair_shards(
    tokens,
    cotangent,
    loss_mask,
    prefix,
    counts,
    w_qkv,
    b_qkv,
    w_dense,
    b_dense,
    ln1_gain,
    ln1_bias,
    w_up,
    b_up,
    w_down,
    b_down,
    ln2_gain,
    ln2_bias,
):
    slots, home_rows, width = tokens.shape[1:]
    n_tensor = lax.axis_size("tensor")
    length = home_rows * n_tensor
    own_count = length // 2
    head_dim = w_qkv.shape[2] // 3
    shard_heads = w_qkv.shape[1]
    heads = 2 * shard_heads
    shard_hidden = w_up.shape[2]
    block_width = w_qkv.shape[0]
    side = lax.axis_index("obj")
    place = lax.axis_index("dp")
    layer = lax.axis_index("tensor")
    item_slot = layer >> 1

    def along(axis, step):
        moves = [(i, i ^ step) for i in range(lax.axis_size(axis))]

        def move(values, gate=()):
            if gate:
                values = after(values, *gate)
            return lax.ppermute(values, axis, moves)

        return move

    over_x = along("obj", 1)
    over_y = along("dp", 2)
    over_core = along("dp", 1)
    swap = along("tensor", 1)
    over_far = along("tensor", 2)

    def to_local(values):
        parts = [
            lax.dynamic_slice_in_dim(values, (place ^ k) * block_width, block_width, -1)
            for k in (0, 2, 1, 3)
        ]
        return jnp.concatenate(parts, axis=-1)

    def from_local(values):
        parts = []
        for g in range(4):
            k = place ^ g
            at = ((k & 1) << 1) | (k >> 1)
            parts.append(lax.dynamic_slice_in_dim(values, at * block_width, block_width, -1))
        return jnp.concatenate(parts, axis=-1)

    def away(values, gate=()):
        stays = lax.dynamic_index_in_dim(values, item_slot, 0, keepdims=False)
        leaves = lax.dynamic_index_in_dim(values, 1 - item_slot, 0, keepdims=False)
        return [stays, over_far(leaves, gate)]

    def home(values, gate=()):
        stays, leaves = values
        came = over_far(leaves, gate)
        first = jnp.where(item_slot == 0, stays, came)
        second = jnp.where(item_slot == 0, came, stays)
        return from_local(jnp.stack([first, second])), came

    def side_first(values, axis=0):
        count = values.shape[axis] // 2
        return (
            lax.dynamic_slice_in_dim(values, side * count, count, axis),
            lax.dynamic_slice_in_dim(values, (1 - side) * count, count, axis),
        )

    def sides(mine, other):
        return jnp.concatenate(
            [jnp.where(side == 0, mine, other), jnp.where(side == 0, other, mine)], axis=0
        )

    latest = []

    def turn(work, first, *rest, wait=()):
        result = work(after(first, *latest, *wait), *rest)
        latest[:] = [result[0] if isinstance(result, (tuple, list)) else result]
        return result

    narrow = jnp.bfloat16
    wide = jnp.float32

    class Gathering:
        def __init__(self, *shards):
            halves = [side_first(shard) for shard in shards]
            self.mine = jnp.concatenate([half[0] for half in halves], axis=0)
            self.rest = jnp.concatenate([half[1] for half in halves], axis=0)
            self.counts = [half[0].shape[0] for half in halves]

        def to_far(self, gate=()):
            self.far = over_far(self.mine, gate)

        def far_to_y(self, gate=()):
            self.far_y = over_y(self.far, gate)

        def far_to_x(self, gate=()):
            self.other_far = over_x(self.far, gate)

        def both_to_x(self, gate=()):
            self.other_far_y = over_x(self.far_y, gate)

        def blocks(self, wait=(), wait_next=()):
            near = [(self.mine, 0), (self.rest, 0), (self.far, 0), (self.other_far, 0)]
            next_y = [self.near_y, self.other_y, (self.far_y, 0), (self.other_far_y, 0)]
            total = 8 * sum(self.counts)
            target = None
            for half, parts in enumerate((near, next_y)):
                first = 0
                for count in self.counts:
                    rest = [(array, start + first) for array, start in parts[1:]]
                    target = turn(
                        lambda array: join(
                            [(array, parts[0][1] + first)] + rest,
                            count,
                            target,
                            total,
                            8 * first + 4 * half * count,
                        ),
                        parts[0][0],
                        wait=(wait, wait_next)[half],
                    )
                    first += count
            self.joined = target, over_core(target)

        def weights(self):
            first = 0
            result = []
            for count in self.counts:
                starts = (8 * first, 8 * first + 4 * count)
                arrays = [(array, start) for array in self.joined for start in starts]
                result.append(Weight(arrays, 4 * count))
                first += count
            return result

    class Reduction:
        def __init__(self, features, rights):
            self.features = features
            self.rights = rights

        def part(self, *given, wait=(), **more):
            array, row, count = self.features[0]
            return turn(
                lambda first: outer(
                    [(first, row, count)] + self.features[1:], self.rights, *given, **more
                ),
                array,
                wait=wait,
            )

        def to_core(self, wait=()):
            (sent,) = self.part(2 * block_width, 2 * block_width, 1, wait=wait)
            self.came = over_core(sent)

        def to_y(self, wait=()):
            sent = self.part(
                block_width, block_width, 2, added=[(self.came, block_width)], wait=wait
            )
            far = over_y(sent[1])
            self.came_y = [over_y(sent[0]), far]

        def to_x(self, wait=()):
            near, near_sent, far, far_sent = self.part(
                0, block_width, 4, added=[(self.came, 0)], pieces=self.came_y, wait=wait
            )
            self.far = (far, over_x(far_sent))
            self.near = (near, over_x(near_sent))

        def to_far(self, gate=()):
            self.came_far = over_far(add(*self.far), gate)

        def finish(self):
            self.mine = add(*self.near, self.came_far)
            self.other = over_x(self.mine)
            return sides(self.mine, self.other).astype(wide)

    class HalfReduction:
        def __init__(self, features, rights):
            self.features = features
            self.rights = rights

        def part(self, *given, wait=(), **more):
            array, row, count = self.features[0]
            return turn(
                lambda first: outer(
                    [(first, row, count)] + self.features[1:],
                    self.rights,
                    *given,
                    steps=1,
                    **more,
                ),
                array,
                wait=wait,
            )

        def to_core(self, wait=()):
            (sent,) = self.part(2 * block_width, 2 * block_width, 1, wait=wait)
            self.came = over_core(sent)

        def to_y(self, wait=()):
            (sent,) = self.part(
                block_width, block_width, 1, added=[(self.came, block_width)], wait=wait
            )
            self.came_y = over_y(sent)

        def to_x(self, wait=()):
            kept, sent = self.part(
                0, block_width, 2, added=[(self.came, 0), (self.came_y, 0)], wait=wait
            )
            self.pair = (kept, over_x(sent))

    def add(*values):
        total = values[0].astype(wide)
        for value in values[1:]:
            total = total + value.astype(wide)
        return total.astype(narrow)

    count_float = counts.astype(jnp.float32)
    share = jnp.where(side == 0, count_float[0], count_float[1]) / (
        count_float[0] + count_float[1]
    )
    limit = jnp.where(side == 0, length, prefix[item_slot]).astype(jnp.int32).reshape(1)

    shard_qkv = w_qkv.reshape(block_width, shard_heads * 3 * head_dim).T
    shard_dense = w_dense.reshape(shard_heads * head_dim, block_width)
    up_rows = jnp.swapaxes(w_up, 1, 2)

    near_bias = jnp.concatenate(
        side_first(b_qkv.reshape(-1))
        + side_first(b_up[0])
        + side_first(b_up[1])
    )
    far_bias = lax.ppermute(near_bias, "tensor", [(i, i ^ 2) for i in range(n_tensor)])
    n_qkv = b_qkv.size

    def bias_row(start, count):
        parts = [near_bias[start : start + count], far_bias[start : start + count]]
        return jnp.concatenate(parts).astype(jnp.float32)[None]

    bias_qkv = bias_row(0, n_qkv)
    bias_gate = bias_row(n_qkv, shard_hidden)
    bias_upper = bias_row(n_qkv + shard_hidden, shard_hidden)

    def row_vector(values):
        return to_local(values.astype(jnp.float32)[None])

    bias_dense = row_vector(b_dense)
    gain_one = row_vector(ln1_gain)
    shift_one = row_vector(ln1_bias)
    bias_down = row_vector(b_down)
    gain_two = row_vector(ln2_gain)
    shift_two = row_vector(ln2_bias)

    share_rows = own_count // CHUNKS

    def positions(owner):
        return owner * home_rows + jnp.arange(home_rows, dtype=jnp.int32)

    where_rows = jnp.concatenate([positions(layer ^ k) for k in (0, 1, 2, 3)])
    key_pos = where_rows[:, None]
    query_pos = where_rows[None, :]
    half_dim = head_dim // 2
    frequency = 10000.0 ** (-2.0 * jnp.arange(half_dim, dtype=jnp.float32) / head_dim)
    angles = where_rows.astype(jnp.float32)[:, None] * frequency[None, :]
    cos_table = jnp.cos(angles)
    cos_table = jnp.concatenate([cos_table, cos_table], axis=1)
    sin_table = jnp.sin(angles)
    sin_table = jnp.concatenate([-sin_table, sin_table], axis=1)

    masked = cotangent[0] * loss_mask[0].astype(jnp.bfloat16)[..., None]
    early = Gathering(shard_qkv, shard_dense)
    middle = Gathering(up_rows[0])
    third = Gathering(up_rows[1])
    late = Gathering(w_down)

    early.to_far((far_bias,))
    early_y = over_y(early.mine)
    leaving = to_local(tokens[0])
    stays = lax.dynamic_index_in_dim(leaving, item_slot, 0, keepdims=False)
    came_tokens = [swap(stays)]
    early_other_y = over_x(early_y)
    early.near_y = early_y, 0
    early.other_y = early_other_y, 0
    others = (middle, third)
    others_mine = jnp.concatenate([part.mine for part in others], axis=0)
    early.far = after(early.far, early_other_y, others_mine, stays, late.mine)
    early.far_to_y()
    early.far_to_x()
    early.both_to_x()
    own_tokens = away(leaving, (early.far,))
    others_y = over_y(others_mine, (early.far,))
    came_tokens.append(swap(own_tokens[1]))
    early.blocks(wait=(came_tokens[0],), wait_next=(own_tokens[1], others_y))
    middle.to_far((came_tokens[1],))
    others_other_y = over_x(others_y, latest)
    late_y = over_y(late.mine, latest)
    first_row = 0
    for part in others:
        part.near_y = others_y, first_row
        part.other_y = others_other_y, first_row
        first_row += part.counts[0]
    full_qkv, full_dense = early.weights()
    token_rows = [part for i in range(CHUNKS) for part in (own_tokens[i], came_tokens[i])]

    def turn_rows(work, pieces, *rest, wait=()):
        return turn(lambda first: work([first] + pieces[1:], *rest), pieces[0], wait=wait)

    projected = turn_rows(project, token_rows, full_qkv, bias_qkv, jnp.float32)

    def attend_heads(first, wait):
        return turn(
            attend,
            projected,
            cos_table,
            sin_table,
            key_pos,
            query_pos,
            limit,
            first,
            shard_heads,
            head_dim,
            wait=wait,
        )

    third.to_far((projected,))
    near_heads = attend_heads(0, (late_y,))
    late_other_y = over_x(late_y, latest)
    late.near_y = late_y, 0
    late.other_y = late_other_y, 0
    middle.far_to_y(latest)
    middle.far_to_x(latest)
    far_heads = attend_heads(shard_heads, (others_other_y, middle.far))
    middle.both_to_x(latest)
    late.to_far(latest)

    step = 2 * share_rows
    half_heads = shard_heads * head_dim
    dense_near = full_dense.rows(0, half_heads)
    dense_far = full_dense.rows(half_heads, half_heads)
    states = [dict() for _ in range(CHUNKS)]

    def normalize(values):
        centred = values - jnp.mean(values, axis=-1, keepdims=True)
        scale = lax.rsqrt(jnp.mean(centred * centred, axis=-1, keepdims=True) + epsilon)
        return centred * scale, scale

    def normalize_back(grad, gain, normal, scale):
        turned = grad * gain
        return scale * (
            turned
            - jnp.mean(turned, axis=-1, keepdims=True)
            - normal * jnp.mean(turned * normal, axis=-1, keepdims=True)
        )

    for i, state in enumerate(states):
        own, other = turn(
            lambda n, f: expand(((n, i, step), dense_near), ((f, i, step), dense_far)),
            near_heads[0],
            far_heads[0],
            wait=(middle.far_y, middle.other_far)
            if i == 0
            else (middle.other_far_y,),
        )
        state["dense"] = own, swap(other)
    third.far_to_y(latest)
    third.far_to_x(latest)
    third.both_to_x(latest)
    for i, state in enumerate(states):
        own, came = state["dense"]
        if i:
            came = after(came, states[0]["norm_bf"])
        attn = own + came.astype(wide) + bias_dense
        first = ALPHA * own_tokens[i].astype(wide) + attn
        normal, scale = normalize(first)
        norm_one = normal * gain_one + shift_one
        norm_bf = norm_one.astype(narrow)
        state["one"] = normal, scale, norm_one
        state["norm_bf"] = norm_bf
        state["came_norm"] = swap(norm_bf, (states[0]["came_norm"],) if i else ())
        state["norm_rows"] = [norm_bf, state["came_norm"]]
    middle.blocks(
        wait=[s["norm_bf"] for s in states]
        + [states[0]["came_norm"], third.far_y, third.other_far, late.far, late_other_y]
    )
    late.far_to_y((states[1]["norm_bf"],))
    late.far_to_x((states[1]["norm_bf"],))
    late.both_to_x(latest)
    own_cotangent = away(to_local(masked), latest)
    third.blocks()
    (full_gate,) = middle.weights()
    (full_upper,) = third.weights()
    late.blocks(wait=(states[1]["came_norm"],))
    (full_down,) = late.weights()
    for i, state in enumerate(states):
        state["ff"] = turn_rows(
            ff_forward,
            state["norm_rows"],
            full_gate,
            full_upper,
            bias_gate,
            bias_upper,
            wait=(own_cotangent[1],) if i == 1 else (),
        )
        own, other = turn(
            lambda r: expand(((r, 0, step), full_down)),
            state["ff"][2],
        )
        state["down"] = own, swap(other)
    for i, state in enumerate(states):
        own, came = state["down"]
        if i:
            came = after(came, states[0]["grad_mlp"])
        mlp = own + came.astype(wide) + bias_down
        normal, scale = normalize(ALPHA * state["one"][2] + mlp)
        state["out"] = (normal * gain_two + shift_two).astype(narrow)
        grad_out = own_cotangent[i].astype(wide) * share
        grad_second = normalize_back(grad_out, gain_two, normal, scale)
        grad_mlp = grad_second.astype(narrow)
        state["second"] = grad_second
        state["grad_mlp"] = grad_mlp
        state["came_mlp"] = swap(grad_mlp, (states[0]["came_mlp"],) if i else ())
        state["mlp_rows"] = [grad_mlp, state["came_mlp"]]
        state["vectors_two"] = (
            jnp.sum(grad_mlp.astype(wide), axis=0),
            jnp.sum(grad_out * normal, axis=0),
            jnp.sum(grad_out, axis=0),
        )


    def back_ff(state, wait=()):
        state["back"] = turn_rows(
            ff_back, state["mlp_rows"], full_down, state["ff"][0], state["ff"][1], wait=wait
        )

    def back_up(state, wait=()):
        own, other = turn(
            lambda g, u: expand(((g, 0, step), full_gate), ((u, 0, step), full_upper)),
            state["back"][0],
            state["back"][1],
            wait=wait,
        )
        state["norm_grad"] = own, swap(other)

    def back_one(state):
        own, came = state["norm_grad"]
        normal, scale, _ = state["one"]
        grad_norm = ALPHA * state["second"] + own + came.astype(wide)
        grad_first = normalize_back(grad_norm, gain_one, normal, scale)
        grad_attn = grad_first.astype(narrow)
        state["first"] = grad_first
        state["grad_attn"] = grad_attn
        state["came_attn"] = swap(grad_attn)
        state["attn_rows"] = [grad_attn, state["came_attn"]]
        state["vectors_one"] = (
            jnp.sum(grad_attn.astype(wide), axis=0),
            jnp.sum(grad_norm * normal, axis=0),
            jnp.sum(grad_norm, axis=0),
        )

    def chunks_of(pick):
        return [(pick(state), 0, step) for state in states]

    def rows_of(name):
        return [piece for state in states for piece in state[name]]

    back_ff(states[0], wait=(states[1]["out"],))
    back_up(states[0], wait=(states[1]["came_mlp"],))
    down = Reduction(chunks_of(lambda s: s["ff"][2]), rows_of("mlp_rows"))
    down.to_core()
    back_ff(states[1])
    down.to_y(wait=(states[0]["norm_grad"][1],))
    back_one(states[0])
    back_up(states[1], wait=(states[0]["grad_attn"],))
    norm_all = rows_of("norm_rows")
    gate = Reduction(chunks_of(lambda s: s["back"][0]), norm_all)
    upper = Reduction(chunks_of(lambda s: s["back"][1]), norm_all)
    gate.to_core()
    layer_out, sent_out = home([s["out"] for s in states], latest)
    upper.to_core()
    back_one(states[1])
    zero_row = jnp.zeros((1, heads * head_dim), wide)

    def back_dense(state, wait=()):
        return turn_rows(project, state["attn_rows"], full_dense, zero_row, narrow, wait=wait)

    context_grads = [back_dense(states[0], wait=(states[1]["norm_grad"][1],))]
    gate.to_y(wait=(states[1]["grad_attn"],))
    down.to_x()
    dense_grads = [
        HalfReduction([(part[0], i, step) for i in range(CHUNKS)], rows_of("attn_rows"))
        for part in (near_heads, far_heads)
    ]
    context_grads.append(back_dense(states[1]))

    def back_heads(saved, first, wait=()):
        return turn_rows(
            attend_back,
            context_grads,
            saved[1],
            saved[2],
            cos_table,
            sin_table,
            key_pos,
            query_pos,
            limit,
            first,
            shard_heads,
            head_dim,
            wait=wait,
        )

    def both_chunks(array):
        return [(array, i, step) for i in range(CHUNKS)]

    grad_far, bias_far = back_heads(far_heads, shard_heads)
    qkv_far = HalfReduction(both_chunks(grad_far), token_rows)
    qkv_far.to_core(wait=(gate.came_y[1], down.far[1], sent_out))
    upper.to_y()
    down.to_far()
    grad_near, bias_near = back_heads(near_heads, 0, wait=(down.near[1],))
    qkv_near = HalfReduction(both_chunks(grad_near), token_rows)
    grad_bias_qkv = jnp.concatenate([bias_near, bias_far], axis=0)
    grad_bias_gate = sum(s["back"][2] for s in states)
    grad_bias_upper = sum(s["back"][3] for s in states)

    def spread(values):
        cut = values.reshape(2, 2, -1)
        whole = jnp.zeros((n_tensor, values.size // 2), jnp.float32)
        whole = lax.dynamic_update_index_in_dim(whole, sides(cut[0, 0], cut[0, 1]), layer, 0)
        whole = lax.dynamic_update_index_in_dim(whole, sides(cut[1, 0], cut[1, 1]), layer ^ 2, 0)
        return whole.reshape(-1)

    stacked = jnp.stack(
        [sum(s[name][i] for s in states) for name in ("vectors_one", "vectors_two") for i in range(3)]
    ).reshape(6, 4, block_width)
    targets = place ^ jnp.arange(4, dtype=jnp.int32)
    targets = (((targets & 1) << 1) | (targets >> 1))[None, :, None]
    ordered = jnp.zeros_like(stacked)
    for position in range(4):
        ordered = jnp.where(targets == position, stacked[:, position : position + 1], ordered)
    vectors = (
        ordered.reshape(6, width),
        spread(grad_bias_qkv),
        spread(grad_bias_gate),
        spread(grad_bias_upper),
    )
    totals = lax.psum(vectors, ("obj", "dp", "tensor"))

    gate.to_x(wait=(qkv_far.came,))
    qkv_near.to_core(wait=(down.came_far,) + vectors)
    qkv_far.to_y()
    sum_down = down.finish()
    half_count = full_qkv.count // 2
    weight_near = full_qkv.rows(0, half_count)
    weight_far = full_qkv.rows(half_count, half_count)

    def back_qkv(i, wait=()):
        own, other = turn(
            lambda n, f: expand(((n, i, step), weight_near), ((f, i, step), weight_far)),
            grad_near,
            grad_far,
            wait=wait,
        )
        states[i]["source"] = own, swap(other)

    back_qkv(1)
    gate.to_far(latest)
    qkv_near.to_y(wait=(upper.came_y[0], gate.near[1]))
    back_qkv(0, wait=(down.other,))
    upper.to_x(wait=(states[1]["source"][1],))
    grad_inputs, _ = home(
        [
            (s["source"][0] + s["source"][1].astype(wide) + ALPHA * s["first"]).astype(narrow)
            for s in states
        ]
    )
    grad_inputs = grad_inputs.astype(wide)
    dense_grads[1].to_core(wait=(gate.came_far,))
    dense_grads[0].to_core()
    qkv_far.to_x(wait=(qkv_far.came_y, states[0]["source"][1]))
    sum_gate = gate.finish()
    dense_grads[1].to_y()
    dense_grads[0].to_y()
    came_qkv = over_far(add(*qkv_far.pair))
    upper.to_far()
    qkv_near.to_x(wait=(qkv_near.came_y,))
    dense_grads[1].to_x()
    dense_grads[0].to_x()
    mine_qkv = add(*qkv_near.pair, came_qkv)
    sum_qkv = sides(mine_qkv, over_x(mine_qkv)).astype(wide)
    sum_upper = upper.finish()
    came_dense = over_far(add(*dense_grads[1].pair))
    mine_dense = add(*dense_grads[0].pair, came_dense)
    sum_dense = sides(mine_dense, over_x(mine_dense)).astype(wide)
    norm_total, total_qkv, total_gate, total_upper = [after(t, mine_dense) for t in totals]

    def own_shard(total, count):
        return lax.dynamic_slice_in_dim(total, layer * count, count)

    bias_total_qkv = own_shard(total_qkv, n_qkv).reshape(b_qkv.shape)
    bias_total_up = jnp.stack(
        [own_shard(total_gate, shard_hidden), own_shard(total_upper, shard_hidden)]
    )

    grad_w_qkv = sum_qkv.T.reshape(w_qkv.shape)
    grad_w_dense = sum_dense.reshape(w_dense.shape)
    grad_w_up = jnp.stack([sum_gate.T, sum_upper.T])
    grad_w_down = sum_down

    return (
        layer_out[None],
        grad_inputs[None],
        grad_w_qkv,
        bias_total_qkv,
        grad_w_dense,
        norm_total[0],
        norm_total[1],
        norm_total[2],
        grad_w_up,
        bias_total_up,
        grad_w_down,
        norm_total[3],
        norm_total[4],
        norm_total[5],
    )


def pair_plan_fits(mesh):
    return mesh.shape["obj"] == 2 and mesh.shape["dp"] == 4 and mesh.shape["tensor"] == 4


def solution(mesh):
    body = pair_shards if pair_plan_fits(mesh) else shards
    return jax.shard_map(
        body,
        mesh=mesh,
        in_specs=(
            P("obj", "dp", "tensor", None),
            P("obj", "dp", "tensor", None),
            P("obj", "dp", "tensor"),
            P("dp"),
            P(),
            P("dp", "tensor", None),
            P("tensor", None),
            P("tensor", None, "dp"),
            P(),
            P(),
            P(),
            P(None, "dp", "tensor"),
            P(None, "tensor"),
            P("tensor", "dp"),
            P(),
            P(),
            P(),
        ),
        out_specs=(
            P("obj", "dp", "tensor", None),
            P("obj", "dp", "tensor", None),
            P("dp", "tensor", None),
            P("tensor", None),
            P("tensor", None, "dp"),
            P(),
            P(),
            P(),
            P(None, "dp", "tensor"),
            P(None, "tensor"),
            P("tensor", "dp"),
            P(),
            P(),
            P(),
        ),
        check_vma=False,
    )
```

```python
import math

import jax
import jax.numpy as jnp
from jax import lax
from jax.experimental import pallas as pl
from jax.experimental.pallas import tpu as pltpu
from jax.sharding import PartitionSpec as P

ALPHA = 48.0**0.5
epsilon = 1e-05


def rotary(source):
    length = source.shape[0]
    half_dim = source.shape[-1] // 2
    frequency = 10000.0 ** (-2.0 * jnp.arange(half_dim, dtype=jnp.float32) / source.shape[-1])
    angles = jnp.arange(length, dtype=jnp.float32)[:, None] * frequency[None, :]
    cosine = jnp.cos(angles)[:, None, :]
    sine_table = jnp.sin(angles)[:, None, :]
    first_half = source[..., :half_dim]
    second = source[..., half_dim:]
    return jnp.concatenate(
        [first_half * cosine - second * sine_table, second * cosine + first_half * sine_table],
        axis=-1,
    )


def rope_pair(query_pre, key_pre):
    return (rotary(query_pre), rotary(key_pre))


def layer_norm(source, gain_vec, shift_vec):
    centred = source - jnp.mean(source, axis=-1, keepdims=True)
    variance = jnp.mean(centred * centred, axis=-1, keepdims=True)
    return centred * lax.rsqrt(variance + epsilon) * gain_vec + shift_vec


def geglu(gate_part, up_part):
    return jax.nn.gelu(gate_part) * up_part


def block_scores(query_block, key_bf, start, prefix_length, score_scale):
    length = key_bf.shape[0]
    scores = (
        jnp.einsum("qhd,khd->hqk", query_block, key_bf, preferred_element_type=jnp.float32)
        * score_scale
    )
    query_pos = start + jnp.arange(query_block.shape[0], dtype=jnp.int32)
    key_pos = jnp.arange(length, dtype=jnp.int32)
    visible = (key_pos[None, :] < prefix_length) | (key_pos[None, :] <= query_pos[:, None])
    return jnp.where(visible[None], scores, -1e30)


def shards(
    tokens,
    cotangent,
    loss_mask,
    prefix,
    counts,
    w_qkv,
    b_qkv,
    w_dense,
    b_dense,
    ln1_gain,
    ln1_bias,
    w_up,
    b_up,
    w_down,
    b_down,
    ln2_gain,
    ln2_bias,
):
    item_count = tokens.shape[1]
    row_count = tokens.shape[2]
    model_width = tokens.shape[3]
    length = row_count * lax.axis_size("tensor")
    local_heads = w_qkv.shape[1]
    head_dim = w_qkv.shape[2] // 3
    local_hidden = w_up.shape[2]
    block_rows = min(512, length)
    score_scale = head_dim ** (-0.5)
    group_id = lax.axis_index("obj")
    count_float = counts.astype(jnp.float32)
    share = jnp.where(group_id == 0, count_float[0], count_float[1]) / (
        count_float[0] + count_float[1]
    )
    bias_qkv = b_qkv.astype(jnp.float32)
    bias_dense = b_dense.astype(jnp.float32)
    gain_one = ln1_gain.astype(jnp.float32)
    shift_one = ln1_bias.astype(jnp.float32)
    bias_up = b_up.astype(jnp.float32)
    bias_down = b_down.astype(jnp.float32)
    gain_two = ln2_gain.astype(jnp.float32)
    shift_two = ln2_bias.astype(jnp.float32)

    def fetch():
        return (
            lax.all_gather(w_qkv, "dp", axis=0, tiled=True),
            lax.all_gather(w_dense, "dp", axis=2, tiled=True),
            lax.all_gather(w_up, "dp", axis=1, tiled=True),
            lax.all_gather(w_down, "dp", axis=1, tiled=True),
        )

    def one_item(item_slot, carry):
        outputs, grad_inputs, large_grads, bias_grads, norm_grads = carry
        qkv_full, dense_full, up_full, down_full = fetch()
        token_rows = lax.dynamic_index_in_dim(tokens[0], item_slot, 0, keepdims=False)
        prefix_length = jnp.where(group_id == 0, length, prefix[item_slot])
        gathered = lax.all_gather(token_rows, "tensor", axis=0, tiled=True)
        projected = (
            jnp.einsum("ld,dhe->lhe", gathered, qkv_full, preferred_element_type=jnp.float32)
            + bias_qkv
        )
        (query_rot, key_rot), rope_pull = jax.vjp(
            rope_pair, projected[..., :head_dim], projected[..., head_dim : 2 * head_dim]
        )
        query_bf = query_rot.astype(jnp.bfloat16)
        key_bf = key_rot.astype(jnp.bfloat16)
        value_bf = projected[..., 2 * head_dim :].astype(jnp.bfloat16)
        context_parts = []
        lse_parts = []
        for start in range(0, length, block_rows):
            scores = block_scores(
                query_bf[start : start + block_rows], key_bf, start, prefix_length, score_scale
            )
            highest_score = jnp.max(scores, axis=-1, keepdims=True)
            expo = jnp.exp(scores - highest_score)
            totals = jnp.sum(expo, axis=-1, keepdims=True)
            soft_weights = (expo / totals).astype(jnp.bfloat16)
            context_parts.append(
                jnp.einsum(
                    "hqk,khd->qhd", soft_weights, value_bf, preferred_element_type=jnp.float32
                )
            )
            lse_parts.append((highest_score + jnp.log(totals))[..., 0])
        context_bf = jnp.concatenate(context_parts, axis=0).astype(jnp.bfloat16)
        log_totals = jnp.concatenate(lse_parts, axis=1)
        source = token_rows.astype(jnp.float32)
        piece = lax.slice_in_dim(context_bf, 0, lax.axis_size("tensor") * row_count, axis=0)
        attn_rows = (
            lax.psum_scatter(
                jnp.einsum("lhd,hde->le", piece, dense_full, preferred_element_type=jnp.float32),
                "tensor",
                scatter_dimension=0,
                tiled=True,
            )
            + bias_dense
        )
        first_norm, norm_one_pull = jax.vjp(
            layer_norm, ALPHA * source + attn_rows, gain_one, shift_one
        )
        norm_full = lax.all_gather(first_norm.astype(jnp.bfloat16), "tensor", axis=0, tiled=True)
        gate_up = (
            jnp.einsum("ld,kdf->klf", norm_full, up_full, preferred_element_type=jnp.float32)
            + bias_up[:, None, :]
        )
        activated, act_pull = jax.vjp(geglu, gate_up[0], gate_up[1])
        hidden_bf = activated.astype(jnp.bfloat16)
        piece = lax.slice_in_dim(hidden_bf, 0, lax.axis_size("tensor") * row_count, axis=0)
        mlp_rows = (
            lax.psum_scatter(
                jnp.dot(piece, down_full, preferred_element_type=jnp.float32),
                "tensor",
                scatter_dimension=0,
                tiled=True,
            )
            + bias_down
        )
        result, norm_two_pull = jax.vjp(
            layer_norm, ALPHA * first_norm + mlp_rows, gain_two, shift_two
        )
        qkv_back, dense_back, up_back, down_back = fetch()
        mask_rows = lax.dynamic_index_in_dim(loss_mask[0], item_slot, 0, keepdims=False).astype(
            jnp.float32
        )
        cot_rows = lax.dynamic_index_in_dim(cotangent[0], item_slot, 0, keepdims=False).astype(
            jnp.float32
        )
        grad_out = cot_rows * mask_rows[:, None] * share
        grad_second, grad_gain_two, grad_shift_two = norm_two_pull(grad_out)
        grad_mlp = grad_second.astype(jnp.bfloat16)
        grad_bias_down = jnp.sum(grad_mlp.astype(jnp.float32), axis=0)
        grad_mlp_full = lax.all_gather(grad_mlp, "tensor", axis=0, tiled=True)
        grad_down = jnp.einsum(
            "lf,ld->fd", hidden_bf, grad_mlp_full, preferred_element_type=jnp.float32
        )
        grad_hidden = jnp.einsum(
            "ld,fd->lf", grad_mlp_full, down_back, preferred_element_type=jnp.float32
        )
        grad_gate, grad_upper = act_pull(grad_hidden)
        grad_gate_up = jnp.stack([grad_gate, grad_upper]).astype(jnp.bfloat16)
        grad_bias_up = jnp.sum(grad_gate_up.astype(jnp.float32), axis=1)
        grad_up = jnp.einsum(
            "ld,klf->kdf", norm_full, grad_gate_up, preferred_element_type=jnp.float32
        )
        piece = lax.slice_in_dim(grad_gate_up, 0, lax.axis_size("tensor") * row_count, axis=1)
        grad_norm_one = ALPHA * grad_second + lax.psum_scatter(
            jnp.einsum("klf,kdf->ld", piece, up_back, preferred_element_type=jnp.float32),
            "tensor",
            scatter_dimension=0,
            tiled=True,
        )
        grad_first, grad_gain_one, grad_shift_one = norm_one_pull(grad_norm_one)
        grad_attn = grad_first.astype(jnp.bfloat16)
        grad_bias_dense = jnp.sum(grad_attn.astype(jnp.float32), axis=0)
        grad_attn_full = lax.all_gather(grad_attn, "tensor", axis=0, tiled=True)
        grad_dense = jnp.einsum(
            "lhd,le->hde", context_bf, grad_attn_full, preferred_element_type=jnp.float32
        )
        grad_context = jnp.einsum(
            "le,hde->lhd", grad_attn_full, dense_back, preferred_element_type=jnp.float32
        ).astype(jnp.bfloat16)
        query_grads = []
        key_grad = jnp.zeros((length, local_heads, head_dim), jnp.float32)
        value_grad = jnp.zeros((length, local_heads, head_dim), jnp.float32)
        for start in range(0, length, block_rows):
            query_block = query_bf[start : start + block_rows]
            scores = block_scores(query_block, key_bf, start, prefix_length, score_scale)
            soft_full = jnp.exp(scores - log_totals[:, start : start + block_rows, None])
            context_block = grad_context[start : start + block_rows]
            grad_soft = jnp.einsum(
                "qhd,khd->hqk", context_block, value_bf, preferred_element_type=jnp.float32
            )
            grad_scores = (
                soft_full * (grad_soft - jnp.sum(soft_full * grad_soft, axis=-1, keepdims=True))
            ).astype(jnp.bfloat16)
            query_grads.append(
                jnp.einsum("hqk,khd->qhd", grad_scores, key_bf, preferred_element_type=jnp.float32)
                * score_scale
            )
            key_grad = (
                key_grad
                + jnp.einsum(
                    "hqk,qhd->khd", grad_scores, query_block, preferred_element_type=jnp.float32
                )
                * score_scale
            )
            value_grad = value_grad + jnp.einsum(
                "hqk,qhd->khd",
                soft_full.astype(jnp.bfloat16),
                context_block,
                preferred_element_type=jnp.float32,
            )
        grad_query_pre, grad_key_pre = rope_pull((jnp.concatenate(query_grads, axis=0), key_grad))
        grad_projected = jnp.concatenate(
            [grad_query_pre, grad_key_pre, value_grad], axis=-1
        ).astype(jnp.bfloat16)
        grad_bias_qkv = jnp.sum(grad_projected.astype(jnp.float32), axis=0)
        grad_qkv = jnp.einsum(
            "ld,lhe->dhe", gathered, grad_projected, preferred_element_type=jnp.float32
        )
        piece = lax.slice_in_dim(grad_projected, 0, row_count * lax.axis_size("tensor"), axis=0)
        grad_source = ALPHA * grad_first + lax.psum_scatter(
            jnp.einsum("lhe,dhe->ld", piece, qkv_back, preferred_element_type=jnp.float32).astype(
                jnp.bfloat16
            ),
            "tensor",
            scatter_dimension=0,
            tiled=True,
        ).astype(jnp.float32)
        outputs = lax.dynamic_update_index_in_dim(
            outputs, result.astype(jnp.bfloat16), item_slot, 0
        )
        grad_inputs = lax.dynamic_update_index_in_dim(grad_inputs, grad_source, item_slot, 0)
        large_grads = (
            large_grads[0] + grad_qkv,
            large_grads[1] + grad_dense,
            large_grads[2] + grad_up,
            large_grads[3] + grad_down,
        )
        bias_grads = (bias_grads[0] + grad_bias_qkv, bias_grads[1] + grad_bias_up)
        norm_grads = (
            norm_grads[0] + grad_bias_dense,
            norm_grads[1] + grad_gain_one,
            norm_grads[2] + grad_shift_one,
            norm_grads[3] + grad_bias_down,
            norm_grads[4] + grad_gain_two,
            norm_grads[5] + grad_shift_two,
        )
        return (outputs, grad_inputs, large_grads, bias_grads, norm_grads)

    zero_vector = jnp.zeros((model_width,), jnp.float32)
    initial = (
        jnp.zeros((item_count, row_count, model_width), jnp.bfloat16),
        jnp.zeros((item_count, row_count, model_width), jnp.float32),
        (
            jnp.zeros((model_width, local_heads, 3 * head_dim), jnp.float32),
            jnp.zeros((local_heads, head_dim, model_width), jnp.float32),
            jnp.zeros((2, model_width, local_hidden), jnp.float32),
            jnp.zeros((local_hidden, model_width), jnp.float32),
        ),
        (
            jnp.zeros((local_heads, 3 * head_dim), jnp.float32),
            jnp.zeros((2, local_hidden), jnp.float32),
        ),
        (zero_vector, zero_vector, zero_vector, zero_vector, zero_vector, zero_vector),
    )
    outputs, grad_inputs, large_grads, bias_grads, norm_grads = lax.fori_loop(
        0, item_count, one_item, initial
    )
    sharded = (
        lax.psum_scatter(
            large_grads[0].astype(jnp.bfloat16), "dp", scatter_dimension=0, tiled=True
        ).astype(jnp.float32),
        lax.psum_scatter(
            large_grads[1].astype(jnp.bfloat16), "dp", scatter_dimension=2, tiled=True
        ).astype(jnp.float32),
        lax.psum_scatter(
            large_grads[2].astype(jnp.bfloat16), "dp", scatter_dimension=1, tiled=True
        ).astype(jnp.float32),
        lax.psum_scatter(
            large_grads[3].astype(jnp.bfloat16), "dp", scatter_dimension=1, tiled=True
        ).astype(jnp.float32),
    )
    merged = (
        lax.psum(sharded[0].astype(jnp.bfloat16), "obj").astype(jnp.float32),
        lax.psum(sharded[1].astype(jnp.bfloat16), "obj").astype(jnp.float32),
        lax.psum(sharded[2].astype(jnp.bfloat16), "obj").astype(jnp.float32),
        lax.psum(sharded[3].astype(jnp.bfloat16), "obj").astype(jnp.float32),
    )
    bias_total = lax.psum((bias_grads[0], bias_grads[1]), ("obj", "dp"))
    norm_total = lax.psum(
        (norm_grads[0], norm_grads[1], norm_grads[2], norm_grads[3], norm_grads[4], norm_grads[5]),
        ("obj", "dp", "tensor"),
    )
    return (
        outputs[None],
        grad_inputs[None],
        merged[0],
        bias_total[0],
        merged[1],
        norm_total[0],
        norm_total[1],
        norm_total[2],
        merged[2],
        bias_total[1],
        merged[3],
        norm_total[3],
        norm_total[4],
        norm_total[5],
    )


def paced(flops):
    return pl.CostEstimate(flops=int(flops / 2), bytes_accessed=1, transcendentals=0)


def attend(projected, cos_table, sin_table, key_pos, query_pos, limit, first, heads, head_dim):
    length = projected.shape[0]
    block = min(256, length)
    score_scale = head_dim ** (-0.5)
    half_dim = head_dim // 2

    def kernel(limit_ref, proj_ref, cos_ref, sin_ref, kpos_ref, qpos_ref, ctx_ref, qkv_ref, lse_ref):
        cosine = cos_ref[...]
        sine = sin_ref[...]
        query = proj_ref[:, :head_dim].astype(jnp.float32)
        key = proj_ref[:, head_dim : 2 * head_dim].astype(jnp.float32)
        query = query * cosine + pltpu.roll(query, half_dim, 1) * sine
        key = key * cosine + pltpu.roll(key, half_dim, 1) * sine
        qkv_ref[:, :head_dim] = query.astype(jnp.bfloat16)
        key_bf = key.astype(jnp.bfloat16)
        qkv_ref[:, head_dim : 2 * head_dim] = key_bf
        value_bf = proj_ref[:, 2 * head_dim :].astype(jnp.bfloat16)
        qkv_ref[:, 2 * head_dim :] = value_bf
        prefix_length = limit_ref[0]
        near = kpos_ref[...] < prefix_length
        for start in range(0, length, block):
            rows = slice(start, start + block)
            scores = (
                lax.dot_general(
                    key_bf,
                    qkv_ref[rows, :head_dim],
                    (((1,), (1,)), ((), ())),
                    preferred_element_type=jnp.float32,
                )
                * score_scale
            )
            visible = near | (kpos_ref[...] <= qpos_ref[:, rows])
            scores = jnp.where(visible, scores, -1e30)
            highest_score = jnp.max(scores, axis=0, keepdims=True)
            expo = jnp.exp(scores - highest_score)
            totals = jnp.sum(expo, axis=0, keepdims=True)
            weights = (expo / totals).astype(jnp.bfloat16)
            ctx_ref[rows, :] = lax.dot_general(
                weights,
                value_bf,
                (((0,), (0,)), ((), ())),
                preferred_element_type=jnp.float32,
            ).astype(jnp.bfloat16)
            lse_ref[0, :, rows] = highest_score + jnp.log(totals)

    fixed = lambda h, lim: (0, 0)
    return pl.pallas_call(
        kernel,
        grid_spec=pltpu.PrefetchScalarGridSpec(
            num_scalar_prefetch=1,
            grid=(heads,),
            in_specs=[
                pl.BlockSpec((length, 3 * head_dim), lambda h, lim: (0, h + first)),
                pl.BlockSpec((length, head_dim), fixed),
                pl.BlockSpec((length, head_dim), fixed),
                pl.BlockSpec((length, 1), fixed),
                pl.BlockSpec((1, length), fixed),
            ],
            out_specs=[
                pl.BlockSpec((length, head_dim), lambda h, lim: (0, h)),
                pl.BlockSpec((length, 3 * head_dim), lambda h, lim: (0, h)),
                pl.BlockSpec((1, 1, length), lambda h, lim: (h, 0, 0)),
            ],
        ),
        out_shape=[
            jax.ShapeDtypeStruct((length, heads * head_dim), jnp.bfloat16),
            jax.ShapeDtypeStruct((length, heads * 3 * head_dim), jnp.bfloat16),
            jax.ShapeDtypeStruct((heads, 1, length), jnp.float32),
        ],
        compiler_params=pltpu.CompilerParams(vmem_limit_bytes=48 * 1024 * 1024),
        cost_estimate=paced(8 * heads * length * length * head_dim),
        name="attend",
    )(limit, projected, cos_table, sin_table, key_pos, query_pos)


def attend_back(
    grad_contexts,
    qkv,
    log_totals,
    cos_table,
    sin_table,
    key_pos,
    query_pos,
    limit,
    first,
    heads,
    head_dim,
):
    length = qkv.shape[0]
    block = min(256, length // 2)
    score_scale = head_dim ** (-0.5)
    half_dim = head_dim // 2

    def kernel(
        limit_ref,
        qkv_ref,
        grad_first,
        grad_second,
        lse_ref,
        cos_ref,
        sin_ref,
        kpos_ref,
        qpos_ref,
        out_ref,
        bias_ref,
        query_grad,
        key_grad,
        value_grad,
    ):
        key_bf = qkv_ref[:, head_dim : 2 * head_dim]
        value_bf = qkv_ref[:, 2 * head_dim :]
        prefix_length = limit_ref[0]
        near = kpos_ref[...] < prefix_length
        for start in range(0, length, block):
            rows = slice(start, start + block)
            query_block = qkv_ref[rows, :head_dim]
            grad_ref = grad_first if start < length // 2 else grad_second
            shift = start % (length // 2)
            grad_block = grad_ref[shift : shift + block, :]
            scores = (
                lax.dot_general(
                    key_bf,
                    query_block,
                    (((1,), (1,)), ((), ())),
                    preferred_element_type=jnp.float32,
                )
                * score_scale
            )
            visible = near | (kpos_ref[...] <= qpos_ref[:, rows])
            soft = jnp.exp(jnp.where(visible, scores, -1e30) - lse_ref[0, :, rows])
            grad_soft = lax.dot_general(
                value_bf,
                grad_block,
                (((1,), (1,)), ((), ())),
                preferred_element_type=jnp.float32,
            )
            inner = jnp.sum(soft * grad_soft, axis=0, keepdims=True)
            grad_scores = (soft * (grad_soft - inner)).astype(jnp.bfloat16)
            query_grad[rows, :] = (
                lax.dot_general(
                    grad_scores,
                    key_bf,
                    (((0,), (0,)), ((), ())),
                    preferred_element_type=jnp.float32,
                )
                * score_scale
            )
            key_term = (
                jnp.dot(grad_scores, query_block, preferred_element_type=jnp.float32) * score_scale
            )
            value_term = jnp.dot(
                soft.astype(jnp.bfloat16), grad_block, preferred_element_type=jnp.float32
            )
            if start == 0:
                key_grad[...] = key_term
                value_grad[...] = value_term
            else:
                key_grad[...] += key_term
                value_grad[...] += value_term
        cosine = cos_ref[...]
        sine = sin_ref[...]
        turned = query_grad[...]
        turned = (turned * cosine + pltpu.roll(turned * sine, half_dim, 1)).astype(jnp.bfloat16)
        out_ref[:, :head_dim] = turned
        bias_ref[0, :, :head_dim] = jnp.sum(turned.astype(jnp.float32), axis=0, keepdims=True)
        turned = key_grad[...]
        turned = (turned * cosine + pltpu.roll(turned * sine, half_dim, 1)).astype(jnp.bfloat16)
        out_ref[:, head_dim : 2 * head_dim] = turned
        bias_ref[0, :, head_dim : 2 * head_dim] = jnp.sum(
            turned.astype(jnp.float32), axis=0, keepdims=True
        )
        turned = value_grad[...].astype(jnp.bfloat16)
        out_ref[:, 2 * head_dim :] = turned
        bias_ref[0, :, 2 * head_dim :] = jnp.sum(turned.astype(jnp.float32), axis=0, keepdims=True)

    fixed = lambda h, lim: (0, 0)
    return pl.pallas_call(
        kernel,
        grid_spec=pltpu.PrefetchScalarGridSpec(
            num_scalar_prefetch=1,
            grid=(heads,),
            in_specs=[
                pl.BlockSpec((length, 3 * head_dim), lambda h, lim: (0, h)),
                pl.BlockSpec((length // 2, head_dim), lambda h, lim: (0, h + first)),
                pl.BlockSpec((length // 2, head_dim), lambda h, lim: (0, h + first)),
                pl.BlockSpec((1, 1, length), lambda h, lim: (h, 0, 0)),
                pl.BlockSpec((length, head_dim), fixed),
                pl.BlockSpec((length, head_dim), fixed),
                pl.BlockSpec((length, 1), fixed),
                pl.BlockSpec((1, length), fixed),
            ],
            out_specs=[
                pl.BlockSpec((length, 3 * head_dim), lambda h, lim: (0, h)),
                pl.BlockSpec((1, 1, 3 * head_dim), lambda h, lim: (h, 0, 0)),
            ],
            scratch_shapes=[pltpu.VMEM((length, head_dim), jnp.float32)] * 3,
        ),
        out_shape=[
            jax.ShapeDtypeStruct((length, heads * 3 * head_dim), jnp.bfloat16),
            jax.ShapeDtypeStruct((heads, 1, 3 * head_dim), jnp.float32),
        ],
        compiler_params=pltpu.CompilerParams(vmem_limit_bytes=48 * 1024 * 1024),
        cost_estimate=paced(10 * heads * length * length * head_dim),
        name="attend_back",
    )(limit, qkv, *grad_contexts, log_totals, cos_table, sin_table, key_pos, query_pos)


def transposed_dot(left, right):
    return lax.dot_general(
        left, right, (((1,), (1,)), ((), ())), preferred_element_type=jnp.float32
    )


def rows_outer(features, right):
    return lax.dot_general(
        features, right, (((0,), (0,)), ((), ())), preferred_element_type=jnp.float32
    )


VMEM_BYTES = 60 * 1024 * 1024


def join(parts, count, target, total, offset):
    width = parts[0][0].shape[1]
    rows = count
    while offset % rows or any(first % rows for _, first in parts):
        rows //= 2
    steps = count // rows

    def kernel(*refs):
        for index in range(4):

            @pl.when(pl.program_id(1) == index)
            def _():
                refs[-1][...] = refs[index][...]

    def source(first):
        return pl.BlockSpec((rows, width), lambda i, p: (first // rows + i, 0))

    given = [] if target is None else [target]
    return pl.pallas_call(
        kernel,
        grid=(steps, 4),
        in_specs=[source(first) for _, first in parts]
        + [pl.BlockSpec(memory_space=pl.ANY)] * len(given),
        out_specs=pl.BlockSpec((rows, width), lambda i, p: (offset // rows + p * steps + i, 0)),
        out_shape=jax.ShapeDtypeStruct((total, width), parts[0][0].dtype),
        input_output_aliases={4: 0} if given else {},
        compiler_params=pltpu.CompilerParams(vmem_limit_bytes=VMEM_BYTES),
        cost_estimate=paced(1000 * count * width),
        name="join",
    )(*[array for array, _ in parts], *given)


def block_of(count, sizes=(512, 256, 128)):
    for size in sizes:
        if count % size == 0:
            return size
    return count


class Weight:
    def __init__(self, arrays, count):
        self.arrays = [array for array, _ in arrays]
        self.starts = [start for _, start in arrays]
        self.count = count
        self.part = self.arrays[0].shape[1]
        self.width = 4 * self.part

    def rows(self, first, count):
        moved = [start + first for start in self.starts]
        return Weight(list(zip(self.arrays, moved)), count)

    def row_specs(self, block):
        def spec(start):
            return pl.BlockSpec((block, self.part), lambda j: (start // block + j, 0))

        return [spec(start) for start in self.starts]


def project_block(rows_ref, weight_refs):
    total = None
    for index, ref in enumerate(weight_refs):
        part = ref.shape[1]
        product = transposed_dot(rows_ref[:, index * part : (index + 1) * part], ref[...])
        total = product if total is None else total + product
    return total


def gather_rows(piece_refs, rows_ref):
    @pl.when(pl.program_id(0) == 0)
    def _():
        row = 0
        for ref in piece_refs:
            rows_ref[row : row + ref.shape[0]] = ref[...]
            row += ref.shape[0]


def piece_specs(pieces):
    return [pl.BlockSpec(piece.shape, lambda j: (0, 0)) for piece in pieces]


def project(pieces, weight, bias, kind):
    width = pieces[0].shape[1]
    count = sum(piece.shape[0] for piece in pieces)
    features = weight.count
    block = block_of(features)
    given = len(pieces)

    def kernel(*refs):
        gather_rows(refs[:given], refs[-1])
        w0, w1, w2, w3, bias_ref, out_ref, rows_ref = refs[given:]
        result = project_block(rows_ref, (w0, w1, w2, w3))
        out_ref[...] = (result + bias_ref[...]).astype(kind)

    return pl.pallas_call(
        kernel,
        grid=(features // block,),
        in_specs=piece_specs(pieces)
        + weight.row_specs(block)
        + [pl.BlockSpec((1, block), lambda j: (0, j))],
        out_specs=pl.BlockSpec((count, block), lambda j: (0, j)),
        out_shape=jax.ShapeDtypeStruct((count, features), kind),
        scratch_shapes=[pltpu.VMEM((count, width), jnp.bfloat16)],
        compiler_params=pltpu.CompilerParams(vmem_limit_bytes=VMEM_BYTES),
        cost_estimate=paced(2 * count * width * features),
        name="project",
    )(*pieces, *weight.arrays, bias)


def ff_forward(pieces, gate_weight, upper_weight, bias_gate, bias_upper):
    width = pieces[0].shape[1]
    count = sum(piece.shape[0] for piece in pieces)
    features = gate_weight.count
    block = block_of(features)
    given = len(pieces)

    def kernel(*refs):
        gather_rows(refs[:given], refs[-1])
        refs = refs[given:]
        bg_ref, bu_ref, gate_ref, upper_ref, hid_ref, rows_ref = refs[8:]
        gate = project_block(rows_ref, refs[:4]) + bg_ref[...]
        upper = project_block(rows_ref, refs[4:8]) + bu_ref[...]
        gate_ref[...] = gate.astype(jnp.bfloat16)
        upper_ref[...] = upper.astype(jnp.bfloat16)
        hid_ref[...] = (jax.nn.gelu(gate) * upper).astype(jnp.bfloat16)

    out = jax.ShapeDtypeStruct((count, features), jnp.bfloat16)
    return pl.pallas_call(
        kernel,
        grid=(features // block,),
        in_specs=piece_specs(pieces)
        + gate_weight.row_specs(block)
        + upper_weight.row_specs(block)
        + [pl.BlockSpec((1, block), lambda j: (0, j))] * 2,
        out_specs=[pl.BlockSpec((count, block), lambda j: (0, j))] * 3,
        out_shape=[out, out, out],
        scratch_shapes=[pltpu.VMEM((count, width), jnp.bfloat16)],
        compiler_params=pltpu.CompilerParams(vmem_limit_bytes=VMEM_BYTES),
        cost_estimate=paced(4 * count * width * features),
        name="ff_forward",
    )(*pieces, *gate_weight.arrays, *upper_weight.arrays, bias_gate, bias_upper)


def ff_back(pieces, down_weight, gate, upper):
    width = pieces[0].shape[1]
    count = sum(piece.shape[0] for piece in pieces)
    features = down_weight.count
    block = features // 2 if features % 256 == 0 else features
    factor = (2.0 / math.pi) ** 0.5
    given = len(pieces)

    def kernel(*refs):
        gather_rows(refs[:given], refs[-1])
        w0, w1, w2, w3, gate_ref, upper_ref, gg_ref, gu_ref, sg_ref, su_ref, rows_ref = refs[given:]
        for start in range(0, block, 512):
            part = slice(start, min(start + 512, block))
            grad = project_block(rows_ref, [ref.at[part] for ref in (w0, w1, w2, w3)])
            value = gate_ref[:, part].astype(jnp.float32)
            square = value * value
            bend = jnp.tanh(factor * value * (1.0 + 0.044715 * square))
            lift = 0.5 * (1.0 + bend)
            slope = lift + 0.5 * value * (1.0 - bend * bend) * (
                factor * (1.0 + 3.0 * 0.044715 * square)
            )
            grad_gate = (grad * upper_ref[:, part].astype(jnp.float32) * slope).astype(jnp.bfloat16)
            grad_upper = (grad * (value * lift)).astype(jnp.bfloat16)
            gg_ref[:, part] = grad_gate
            gu_ref[:, part] = grad_upper
            sg_ref[:, part] = jnp.sum(grad_gate.astype(jnp.float32), axis=0, keepdims=True)
            su_ref[:, part] = jnp.sum(grad_upper.astype(jnp.float32), axis=0, keepdims=True)

    out = jax.ShapeDtypeStruct((count, features), jnp.bfloat16)
    row = jax.ShapeDtypeStruct((1, features), jnp.float32)
    return pl.pallas_call(
        kernel,
        grid=(features // block,),
        in_specs=piece_specs(pieces)
        + down_weight.row_specs(block)
        + [pl.BlockSpec((count, block), lambda j: (0, j))] * 2,
        out_specs=[pl.BlockSpec((count, block), lambda j: (0, j))] * 2
        + [pl.BlockSpec((1, block), lambda j: (0, j))] * 2,
        out_shape=[out, out, row, row],
        scratch_shapes=[pltpu.VMEM((count, width), jnp.bfloat16)],
        compiler_params=pltpu.CompilerParams(vmem_limit_bytes=VMEM_BYTES),
        cost_estimate=paced(3 * count * width * features),
        name="ff_back",
    )(*pieces, *down_weight.arrays, gate, upper)


def expand(*pairs):
    count = pairs[0][0][2]
    width = pairs[0][1].width
    part = width // 4
    own = count // 2
    terms = len(pairs)
    cuts = 2 if sum(weight.count for _, weight in pairs) > 4000 else 1
    block = part // cuts

    def kernel(*refs):
        own_ref, other_ref = refs[5 * terms :]
        for which in range(4):

            @pl.when(pl.program_id(0) // cuts == which)
            def _():
                total = None
                for term in range(terms):
                    product = jnp.dot(
                        refs[5 * term][...],
                        refs[5 * term + 1 + which][...],
                        preferred_element_type=jnp.float32,
                    )
                    total = product if total is None else total + product
                own_ref[...] = total[:own]
                other_ref[...] = total[own:].astype(jnp.bfloat16)

    def column(weight, which):
        return pl.BlockSpec(
            (weight.count, block),
            lambda j: (
                weight.starts[which] // weight.count,
                jnp.clip(j - cuts * which, 0, cuts - 1),
            ),
        )

    specs = []
    operands = []
    def row_block(depth, row):
        return pl.BlockSpec((count, depth), lambda j: (row, 0))

    for (features, row, _), weight in pairs:
        specs.append(row_block(weight.count, row))
        specs += [column(weight, which) for which in range(4)]
        operands += [features, *weight.arrays]
    return pl.pallas_call(
        kernel,
        grid=(4 * cuts,),
        in_specs=specs,
        out_specs=[pl.BlockSpec((own, block), lambda j: (0, j))] * 2,
        out_shape=[
            jax.ShapeDtypeStruct((own, width), jnp.float32),
            jax.ShapeDtypeStruct((own, width), jnp.bfloat16),
        ],
        compiler_params=pltpu.CompilerParams(vmem_limit_bytes=VMEM_BYTES),
        cost_estimate=paced(2 * count * width * sum(weight.count for _, weight in pairs)),
        name="expand",
    )(*operands)


def outer(features, rights, start, columns, parts, added=(), pieces=(), steps=2):
    chunks = len(features)
    count = features[0][2]
    given = len(rights)
    total = features[0][0].shape[1]
    block = total // steps
    rows = total // parts

    def kernel(*refs):
        gather_rows(refs[chunks : chunks + given], refs[-1])
        result = None
        for chunk in range(chunks):
            rows_here = refs[-1][chunk * count : (chunk + 1) * count]
            product = rows_outer(refs[chunk][...], rows_here)
            result = product if result is None else result + product
        first = chunks + given
        for ref in refs[first : first + len(added)]:
            result = result + ref[...].astype(jnp.float32)
        first += len(added)
        outs = refs[first + len(pieces) : -1]
        if parts == 1:
            outs[0][...] = result.astype(jnp.bfloat16)
            return
        each = parts // steps
        for half in range(steps):

            @pl.when(pl.program_id(0) == half)
            def _():
                whole = result
                if pieces:
                    whole = whole + refs[first + half][...].astype(jnp.float32)
                whole = whole.astype(jnp.bfloat16)
                for index in range(each):
                    outs[half * each + index][...] = whole[index * rows : (index + 1) * rows]

    def at(row, column):
        return lambda j: (row, column)

    def across(row):
        return lambda j: (row, j)

    def along(column):
        return lambda j: (j, column)

    if parts == 1:
        out_specs = [pl.BlockSpec((block, columns), along(0))]
    else:
        out_specs = [pl.BlockSpec((rows, columns), at(0, 0))] * parts
    return pl.pallas_call(
        kernel,
        grid=(steps,),
        in_specs=[pl.BlockSpec((count, block), across(row)) for _, row, _ in features]
        + [pl.BlockSpec((right.shape[0], columns), at(0, start // columns)) for right in rights]
        + [pl.BlockSpec((block, columns), along(column // columns)) for _, column in added]
        + [pl.BlockSpec((block, columns), at(0, 0))] * len(pieces),
        out_specs=out_specs,
        out_shape=[jax.ShapeDtypeStruct((rows, columns), jnp.bfloat16)] * parts,
        scratch_shapes=[pltpu.VMEM((chunks * count, columns), jnp.bfloat16)],
        compiler_params=pltpu.CompilerParams(vmem_limit_bytes=VMEM_BYTES),
        cost_estimate=paced(6 * chunks * count * total * columns),
        name="outer",
    )(
        *[array for array, _, _ in features],
        *rights,
        *[array for array, _ in added],
        *pieces,
    )


def after(values, *earlier):
    return lax.optimization_barrier((values,) + earlier)[0]


CHUNKS = 2


def pair_shards(
    tokens,
    cotangent,
    loss_mask,
    prefix,
    counts,
    w_qkv,
    b_qkv,
    w_dense,
    b_dense,
    ln1_gain,
    ln1_bias,
    w_up,
    b_up,
    w_down,
    b_down,
    ln2_gain,
    ln2_bias,
):
    slots, home_rows, width = tokens.shape[1:]
    n_tensor = lax.axis_size("tensor")
    length = home_rows * n_tensor
    own_count = length // 2
    head_dim = w_qkv.shape[2] // 3
    shard_heads = w_qkv.shape[1]
    heads = 2 * shard_heads
    shard_hidden = w_up.shape[2]
    block_width = w_qkv.shape[0]
    side = lax.axis_index("obj")
    place = lax.axis_index("dp")
    layer = lax.axis_index("tensor")
    item_slot = layer >> 1

    def along(axis, step):
        moves = [(i, i ^ step) for i in range(lax.axis_size(axis))]

        def move(values, gate=()):
            if gate:
                values = after(values, *gate)
            return lax.ppermute(values, axis, moves)

        return move

    over_x = along("obj", 1)
    over_y = along("dp", 2)
    over_core = along("dp", 1)
    swap = along("tensor", 1)
    over_far = along("tensor", 2)

    def to_local(values):
        parts = [
            lax.dynamic_slice_in_dim(values, (place ^ k) * block_width, block_width, -1)
            for k in (0, 2, 1, 3)
        ]
        return jnp.concatenate(parts, axis=-1)

    def from_local(values):
        parts = []
        for g in range(4):
            k = place ^ g
            at = ((k & 1) << 1) | (k >> 1)
            parts.append(lax.dynamic_slice_in_dim(values, at * block_width, block_width, -1))
        return jnp.concatenate(parts, axis=-1)

    def away(values, gate=()):
        stays = lax.dynamic_index_in_dim(values, item_slot, 0, keepdims=False)
        leaves = lax.dynamic_index_in_dim(values, 1 - item_slot, 0, keepdims=False)
        return [stays, over_far(leaves, gate)]

    def home(values, gate=()):
        stays, leaves = values
        came = over_far(leaves, gate)
        first = jnp.where(item_slot == 0, stays, came)
        second = jnp.where(item_slot == 0, came, stays)
        return from_local(jnp.stack([first, second])), came

    def side_first(values, axis=0):
        count = values.shape[axis] // 2
        return (
            lax.dynamic_slice_in_dim(values, side * count, count, axis),
            lax.dynamic_slice_in_dim(values, (1 - side) * count, count, axis),
        )

    def sides(mine, other):
        return jnp.concatenate(
            [jnp.where(side == 0, mine, other), jnp.where(side == 0, other, mine)], axis=0
        )

    latest = []

    def turn(work, first, *rest, wait=()):
        result = work(after(first, *latest, *wait), *rest)
        latest[:] = [result[0] if isinstance(result, (tuple, list)) else result]
        return result

    narrow = jnp.bfloat16
    wide = jnp.float32

    class Gathering:
        def __init__(self, *shards):
            halves = [side_first(shard) for shard in shards]
            self.mine = jnp.concatenate([half[0] for half in halves], axis=0)
            self.rest = jnp.concatenate([half[1] for half in halves], axis=0)
            self.counts = [half[0].shape[0] for half in halves]

        def to_far(self, gate=()):
            self.far = over_far(self.mine, gate)

        def far_to_y(self, gate=()):
            self.far_y = over_y(self.far, gate)

        def far_to_x(self, gate=()):
            self.other_far = over_x(self.far, gate)

        def both_to_x(self, gate=()):
            self.other_far_y = over_x(self.far_y, gate)

        def blocks(self, wait=(), wait_next=()):
            near = [(self.mine, 0), (self.rest, 0), (self.far, 0), (self.other_far, 0)]
            next_y = [self.near_y, self.other_y, (self.far_y, 0), (self.other_far_y, 0)]
            total = 8 * sum(self.counts)
            target = None
            for half, parts in enumerate((near, next_y)):
                first = 0
                for count in self.counts:
                    rest = [(array, start + first) for array, start in parts[1:]]
                    target = turn(
                        lambda array: join(
                            [(array, parts[0][1] + first)] + rest,
                            count,
                            target,
                            total,
                            8 * first + 4 * half * count,
                        ),
                        parts[0][0],
                        wait=(wait, wait_next)[half],
                    )
                    first += count
            self.joined = target, over_core(target)

        def weights(self):
            first = 0
            result = []
            for count in self.counts:
                starts = (8 * first, 8 * first + 4 * count)
                arrays = [(array, start) for array in self.joined for start in starts]
                result.append(Weight(arrays, 4 * count))
                first += count
            return result

    class Reduction:
        def __init__(self, features, rights):
            self.features = features
            self.rights = rights

        def part(self, *given, wait=(), **more):
            array, row, count = self.features[0]
            return turn(
                lambda first: outer(
                    [(first, row, count)] + self.features[1:], self.rights, *given, **more
                ),
                array,
                wait=wait,
            )

        def to_core(self, wait=()):
            (sent,) = self.part(2 * block_width, 2 * block_width, 1, wait=wait)
            self.came = over_core(sent)

        def to_y(self, wait=()):
            sent = self.part(
                block_width, block_width, 2, added=[(self.came, block_width)], wait=wait
            )
            far = over_y(sent[1])
            self.came_y = [over_y(sent[0]), far]

        def to_x(self, wait=()):
            near, near_sent, far, far_sent = self.part(
                0, block_width, 4, added=[(self.came, 0)], pieces=self.came_y, wait=wait
            )
            self.far = (far, over_x(far_sent))
            self.near = (near, over_x(near_sent))

        def to_far(self, gate=()):
            self.came_far = over_far(add(*self.far), gate)

        def finish(self):
            self.mine = add(*self.near, self.came_far)
            self.other = over_x(self.mine)
            return sides(self.mine, self.other).astype(wide)

    class HalfReduction:
        def __init__(self, features, rights):
            self.features = features
            self.rights = rights

        def part(self, *given, wait=(), **more):
            array, row, count = self.features[0]
            return turn(
                lambda first: outer(
                    [(first, row, count)] + self.features[1:],
                    self.rights,
                    *given,
                    steps=1,
                    **more,
                ),
                array,
                wait=wait,
            )

        def to_core(self, wait=()):
            (sent,) = self.part(2 * block_width, 2 * block_width, 1, wait=wait)
            self.came = over_core(sent)

        def to_y(self, wait=()):
            (sent,) = self.part(
                block_width, block_width, 1, added=[(self.came, block_width)], wait=wait
            )
            self.came_y = over_y(sent)

        def to_x(self, wait=()):
            kept, sent = self.part(
                0, block_width, 2, added=[(self.came, 0), (self.came_y, 0)], wait=wait
            )
            self.pair = (kept, over_x(sent))

    def add(*values):
        total = values[0].astype(wide)
        for value in values[1:]:
            total = total + value.astype(wide)
        return total.astype(narrow)

    count_float = counts.astype(jnp.float32)
    share = jnp.where(side == 0, count_float[0], count_float[1]) / (
        count_float[0] + count_float[1]
    )
    limit = jnp.where(side == 0, length, prefix[item_slot]).astype(jnp.int32).reshape(1)

    shard_qkv = w_qkv.reshape(block_width, shard_heads * 3 * head_dim).T
    shard_dense = w_dense.reshape(shard_heads * head_dim, block_width)
    up_rows = jnp.swapaxes(w_up, 1, 2)

    near_bias = jnp.concatenate(
        side_first(b_qkv.reshape(-1))
        + side_first(b_up[0])
        + side_first(b_up[1])
    )
    far_bias = lax.ppermute(near_bias, "tensor", [(i, i ^ 2) for i in range(n_tensor)])
    n_qkv = b_qkv.size

    def bias_row(start, count):
        parts = [near_bias[start : start + count], far_bias[start : start + count]]
        return jnp.concatenate(parts).astype(jnp.float32)[None]

    bias_qkv = bias_row(0, n_qkv)
    bias_gate = bias_row(n_qkv, shard_hidden)
    bias_upper = bias_row(n_qkv + shard_hidden, shard_hidden)

    def row_vector(values):
        return to_local(values.astype(jnp.float32)[None])

    bias_dense = row_vector(b_dense)
    gain_one = row_vector(ln1_gain)
    shift_one = row_vector(ln1_bias)
    bias_down = row_vector(b_down)
    gain_two = row_vector(ln2_gain)
    shift_two = row_vector(ln2_bias)

    share_rows = own_count // CHUNKS

    def positions(owner):
        return owner * home_rows + jnp.arange(home_rows, dtype=jnp.int32)

    where_rows = jnp.concatenate([positions(layer ^ k) for k in (0, 1, 2, 3)])
    key_pos = where_rows[:, None]
    query_pos = where_rows[None, :]
    half_dim = head_dim // 2
    frequency = 10000.0 ** (-2.0 * jnp.arange(half_dim, dtype=jnp.float32) / head_dim)
    angles = where_rows.astype(jnp.float32)[:, None] * frequency[None, :]
    cos_table = jnp.cos(angles)
    cos_table = jnp.concatenate([cos_table, cos_table], axis=1)
    sin_table = jnp.sin(angles)
    sin_table = jnp.concatenate([-sin_table, sin_table], axis=1)

    masked = cotangent[0] * loss_mask[0].astype(jnp.bfloat16)[..., None]
    early = Gathering(shard_qkv, shard_dense)
    middle = Gathering(up_rows[0])
    third = Gathering(up_rows[1])
    late = Gathering(w_down)

    early.to_far((far_bias,))
    early_y = over_y(early.mine)
    leaving = to_local(tokens[0])
    stays = lax.dynamic_index_in_dim(leaving, item_slot, 0, keepdims=False)
    came_tokens = [swap(stays)]
    early_other_y = over_x(early_y)
    early.near_y = early_y, 0
    early.other_y = early_other_y, 0
    others = (middle, third)
    others_mine = jnp.concatenate([part.mine for part in others], axis=0)
    early.far = after(early.far, early_other_y, others_mine, stays, late.mine)
    early.far_to_y()
    early.far_to_x()
    early.both_to_x()
    own_tokens = away(leaving, (early.far,))
    others_y = over_y(others_mine, (early.far,))
    came_tokens.append(swap(own_tokens[1]))
    early.blocks(wait=(came_tokens[0],), wait_next=(own_tokens[1], others_y))
    middle.to_far((came_tokens[1],))
    others_other_y = over_x(others_y, latest)
    late_y = over_y(late.mine, latest)
    first_row = 0
    for part in others:
        part.near_y = others_y, first_row
        part.other_y = others_other_y, first_row
        first_row += part.counts[0]
    full_qkv, full_dense = early.weights()
    token_rows = [part for i in range(CHUNKS) for part in (own_tokens[i], came_tokens[i])]

    def turn_rows(work, pieces, *rest, wait=()):
        return turn(lambda first: work([first] + pieces[1:], *rest), pieces[0], wait=wait)

    projected = turn_rows(project, token_rows, full_qkv, bias_qkv, jnp.float32)

    def attend_heads(first, wait):
        return turn(
            attend,
            projected,
            cos_table,
            sin_table,
            key_pos,
            query_pos,
            limit,
            first,
            shard_heads,
            head_dim,
            wait=wait,
        )

    third.to_far((projected,))
    near_heads = attend_heads(0, (late_y,))
    late_other_y = over_x(late_y, latest)
    late.near_y = late_y, 0
    late.other_y = late_other_y, 0
    middle.far_to_y(latest)
    middle.far_to_x(latest)
    far_heads = attend_heads(shard_heads, (others_other_y, middle.far))
    middle.both_to_x(latest)
    late.to_far(latest)

    step = 2 * share_rows
    half_heads = shard_heads * head_dim
    dense_near = full_dense.rows(0, half_heads)
    dense_far = full_dense.rows(half_heads, half_heads)
    states = [dict() for _ in range(CHUNKS)]

    def normalize(values):
        centred = values - jnp.mean(values, axis=-1, keepdims=True)
        scale = lax.rsqrt(jnp.mean(centred * centred, axis=-1, keepdims=True) + epsilon)
        return centred * scale, scale

    def normalize_back(grad, gain, normal, scale):
        turned = grad * gain
        return scale * (
            turned
            - jnp.mean(turned, axis=-1, keepdims=True)
            - normal * jnp.mean(turned * normal, axis=-1, keepdims=True)
        )

    for i, state in enumerate(states):
        own, other = turn(
            lambda n, f: expand(((n, i, step), dense_near), ((f, i, step), dense_far)),
            near_heads[0],
            far_heads[0],
            wait=(middle.far_y, middle.other_far)
            if i == 0
            else (middle.other_far_y,),
        )
        state["dense"] = own, swap(other)
    third.far_to_y(latest)
    third.far_to_x(latest)
    third.both_to_x(latest)
    for i, state in enumerate(states):
        own, came = state["dense"]
        if i:
            came = after(came, states[0]["norm_bf"])
        attn = own + came.astype(wide) + bias_dense
        first = ALPHA * own_tokens[i].astype(wide) + attn
        normal, scale = normalize(first)
        norm_one = normal * gain_one + shift_one
        norm_bf = norm_one.astype(narrow)
        state["one"] = normal, scale, norm_one
        state["norm_bf"] = norm_bf
        state["came_norm"] = swap(norm_bf, (states[0]["came_norm"],) if i else ())
        state["norm_rows"] = [norm_bf, state["came_norm"]]
    middle.blocks(
        wait=[s["norm_bf"] for s in states]
        + [states[0]["came_norm"], third.far_y, third.other_far, late.far, late_other_y]
    )
    late.far_to_y((states[1]["norm_bf"],))
    late.far_to_x((states[1]["norm_bf"],))
    late.both_to_x(latest)
    own_cotangent = away(to_local(masked), latest)
    third.blocks()
    (full_gate,) = middle.weights()
    (full_upper,) = third.weights()
    late.blocks(wait=(states[1]["came_norm"],))
    (full_down,) = late.weights()
    for i, state in enumerate(states):
        state["ff"] = turn_rows(
            ff_forward,
            state["norm_rows"],
            full_gate,
            full_upper,
            bias_gate,
            bias_upper,
            wait=(own_cotangent[1],) if i == 1 else (),
        )
        own, other = turn(
            lambda r: expand(((r, 0, step), full_down)),
            state["ff"][2],
        )
        state["down"] = own, swap(other)
    for i, state in enumerate(states):
        own, came = state["down"]
        if i:
            came = after(came, states[0]["grad_mlp"])
        mlp = own + came.astype(wide) + bias_down
        normal, scale = normalize(ALPHA * state["one"][2] + mlp)
        state["out"] = (normal * gain_two + shift_two).astype(narrow)
        grad_out = own_cotangent[i].astype(wide) * share
        grad_second = normalize_back(grad_out, gain_two, normal, scale)
        grad_mlp = grad_second.astype(narrow)
        state["second"] = grad_second
        state["grad_mlp"] = grad_mlp
        state["came_mlp"] = swap(grad_mlp, (states[0]["came_mlp"],) if i else ())
        state["mlp_rows"] = [grad_mlp, state["came_mlp"]]
        state["vectors_two"] = (
            jnp.sum(grad_mlp.astype(wide), axis=0),
            jnp.sum(grad_out * normal, axis=0),
            jnp.sum(grad_out, axis=0),
        )


    def back_ff(state, wait=()):
        state["back"] = turn_rows(
            ff_back, state["mlp_rows"], full_down, state["ff"][0], state["ff"][1], wait=wait
        )

    def back_up(state, wait=()):
        own, other = turn(
            lambda g, u: expand(((g, 0, step), full_gate), ((u, 0, step), full_upper)),
            state["back"][0],
            state["back"][1],
            wait=wait,
        )
        state["norm_grad"] = own, swap(other)

    def back_one(state):
        own, came = state["norm_grad"]
        normal, scale, _ = state["one"]
        grad_norm = ALPHA * state["second"] + own + came.astype(wide)
        grad_first = normalize_back(grad_norm, gain_one, normal, scale)
        grad_attn = grad_first.astype(narrow)
        state["first"] = grad_first
        state["grad_attn"] = grad_attn
        state["came_attn"] = swap(grad_attn)
        state["attn_rows"] = [grad_attn, state["came_attn"]]
        state["vectors_one"] = (
            jnp.sum(grad_attn.astype(wide), axis=0),
            jnp.sum(grad_norm * normal, axis=0),
            jnp.sum(grad_norm, axis=0),
        )

    def chunks_of(pick):
        return [(pick(state), 0, step) for state in states]

    def rows_of(name):
        return [piece for state in states for piece in state[name]]

    back_ff(states[0], wait=(states[1]["out"],))
    back_up(states[0], wait=(states[1]["came_mlp"],))
    down = Reduction(chunks_of(lambda s: s["ff"][2]), rows_of("mlp_rows"))
    down.to_core()
    back_ff(states[1])
    down.to_y(wait=(states[0]["norm_grad"][1],))
    back_one(states[0])
    back_up(states[1], wait=(states[0]["grad_attn"],))
    norm_all = rows_of("norm_rows")
    gate = Reduction(chunks_of(lambda s: s["back"][0]), norm_all)
    upper = Reduction(chunks_of(lambda s: s["back"][1]), norm_all)
    gate.to_core()
    layer_out, sent_out = home([s["out"] for s in states], latest)
    upper.to_core()
    back_one(states[1])
    zero_row = jnp.zeros((1, heads * head_dim), wide)

    def back_dense(state, wait=()):
        return turn_rows(project, state["attn_rows"], full_dense, zero_row, narrow, wait=wait)

    context_grads = [back_dense(states[0], wait=(states[1]["norm_grad"][1],))]
    gate.to_y(wait=(states[1]["grad_attn"],))
    down.to_x()
    dense_grads = [
        HalfReduction([(part[0], i, step) for i in range(CHUNKS)], rows_of("attn_rows"))
        for part in (near_heads, far_heads)
    ]
    context_grads.append(back_dense(states[1]))

    def back_heads(saved, first, wait=()):
        return turn_rows(
            attend_back,
            context_grads,
            saved[1],
            saved[2],
            cos_table,
            sin_table,
            key_pos,
            query_pos,
            limit,
            first,
            shard_heads,
            head_dim,
            wait=wait,
        )

    def both_chunks(array):
        return [(array, i, step) for i in range(CHUNKS)]

    grad_far, bias_far = back_heads(far_heads, shard_heads)
    qkv_far = HalfReduction(both_chunks(grad_far), token_rows)
    qkv_far.to_core(wait=(gate.came_y[1], down.far[1], sent_out))
    upper.to_y()
    down.to_far()
    grad_near, bias_near = back_heads(near_heads, 0, wait=(down.near[1],))
    qkv_near = HalfReduction(both_chunks(grad_near), token_rows)
    grad_bias_qkv = jnp.concatenate([bias_near, bias_far], axis=0)
    grad_bias_gate = sum(s["back"][2] for s in states)
    grad_bias_upper = sum(s["back"][3] for s in states)

    def spread(values):
        cut = values.reshape(2, 2, -1)
        whole = jnp.zeros((n_tensor, values.size // 2), jnp.float32)
        whole = lax.dynamic_update_index_in_dim(whole, sides(cut[0, 0], cut[0, 1]), layer, 0)
        whole = lax.dynamic_update_index_in_dim(whole, sides(cut[1, 0], cut[1, 1]), layer ^ 2, 0)
        return whole.reshape(-1)

    stacked = jnp.stack(
        [sum(s[name][i] for s in states) for name in ("vectors_one", "vectors_two") for i in range(3)]
    ).reshape(6, 4, block_width)
    targets = place ^ jnp.arange(4, dtype=jnp.int32)
    targets = (((targets & 1) << 1) | (targets >> 1))[None, :, None]
    ordered = jnp.zeros_like(stacked)
    for position in range(4):
        ordered = jnp.where(targets == position, stacked[:, position : position + 1], ordered)
    vectors = (
        ordered.reshape(6, width),
        spread(grad_bias_qkv),
        spread(grad_bias_gate),
        spread(grad_bias_upper),
    )
    totals = lax.psum(vectors, ("obj", "dp", "tensor"))

    gate.to_x(wait=(qkv_far.came,))
    qkv_near.to_core(wait=(down.came_far,) + vectors)
    qkv_far.to_y()
    sum_down = down.finish()
    half_count = full_qkv.count // 2
    weight_near = full_qkv.rows(0, half_count)
    weight_far = full_qkv.rows(half_count, half_count)

    def back_qkv(i, wait=()):
        own, other = turn(
            lambda n, f: expand(((n, i, step), weight_near), ((f, i, step), weight_far)),
            grad_near,
            grad_far,
            wait=wait,
        )
        states[i]["source"] = own, swap(other)

    back_qkv(1)
    gate.to_far(latest)
    qkv_near.to_y(wait=(upper.came_y[0], gate.near[1]))
    back_qkv(0, wait=(down.other,))
    upper.to_x(wait=(states[1]["source"][1],))
    grad_inputs, _ = home(
        [
            (s["source"][0] + s["source"][1].astype(wide) + ALPHA * s["first"]).astype(narrow)
            for s in states
        ]
    )
    grad_inputs = grad_inputs.astype(wide)
    qkv_far.to_x(wait=(qkv_far.came_y, states[0]["source"][1]))
    dense_grads[1].to_core(wait=(gate.came_far,))
    dense_grads[0].to_core()
    sum_gate = gate.finish()
    dense_grads[1].to_y()
    dense_grads[0].to_y()
    came_qkv = over_far(add(*qkv_far.pair))
    upper.to_far()
    qkv_near.to_x(wait=(qkv_near.came_y,))
    dense_grads[1].to_x()
    dense_grads[0].to_x()
    mine_qkv = add(*qkv_near.pair, came_qkv)
    sum_qkv = sides(mine_qkv, over_x(mine_qkv)).astype(wide)
    sum_upper = upper.finish()
    came_dense = over_far(add(*dense_grads[1].pair))
    mine_dense = add(*dense_grads[0].pair, came_dense)
    sum_dense = sides(mine_dense, over_x(mine_dense)).astype(wide)
    norm_total, total_qkv, total_gate, total_upper = [after(t, mine_dense) for t in totals]

    def own_shard(total, count):
        return lax.dynamic_slice_in_dim(total, layer * count, count)

    bias_total_qkv = own_shard(total_qkv, n_qkv).reshape(b_qkv.shape)
    bias_total_up = jnp.stack(
        [own_shard(total_gate, shard_hidden), own_shard(total_upper, shard_hidden)]
    )

    grad_w_qkv = sum_qkv.T.reshape(w_qkv.shape)
    grad_w_dense = sum_dense.reshape(w_dense.shape)
    grad_w_up = jnp.stack([sum_gate.T, sum_upper.T])
    grad_w_down = sum_down

    return (
        layer_out[None],
        grad_inputs[None],
        grad_w_qkv,
        bias_total_qkv,
        grad_w_dense,
        norm_total[0],
        norm_total[1],
        norm_total[2],
        grad_w_up,
        bias_total_up,
        grad_w_down,
        norm_total[3],
        norm_total[4],
        norm_total[5],
    )


def pair_plan_fits(mesh):
    return mesh.shape["obj"] == 2 and mesh.shape["dp"] == 4 and mesh.shape["tensor"] == 4


def solution(mesh):
    body = pair_shards if pair_plan_fits(mesh) else shards
    return jax.shard_map(
        body,
        mesh=mesh,
        in_specs=(
            P("obj", "dp", "tensor", None),
            P("obj", "dp", "tensor", None),
            P("obj", "dp", "tensor"),
            P("dp"),
            P(),
            P("dp", "tensor", None),
            P("tensor", None),
            P("tensor", None, "dp"),
            P(),
            P(),
            P(),
            P(None, "dp", "tensor"),
            P(None, "tensor"),
            P("tensor", "dp"),
            P(),
            P(),
            P(),
        ),
        out_specs=(
            P("obj", "dp", "tensor", None),
            P("obj", "dp", "tensor", None),
            P("dp", "tensor", None),
            P("tensor", None),
            P("tensor", None, "dp"),
            P(),
            P(),
            P(),
            P(None, "dp", "tensor"),
            P(None, "tensor"),
            P("tensor", "dp"),
            P(),
            P(),
            P(),
        ),
        check_vma=False,
    )
```
